32 devices in a mesh: seq: 16 (over z, y, x), head: 2 (over core).
Axes of the slice: x: 2, y: 2, z: 4, core: 2. Of those that a mesh axis runs over, the one named last changes fastest.
Arguments:
- queries: bfloat16 [2048, 6144], P('seq', 'head'), may hold values from -6 to 6
- key_vectors: bfloat16 [2048, 6144], P('seq', 'head'), may hold values from -6 to 6
- value_vectors: bfloat16 [2048, 6144], P('seq', 'head'), may hold values from -6 to 6
- norm_gain: float32 [6144], P('head'), may hold values from 0.1 to 1.9
- upstream: bfloat16 [2048, 6144], P('seq', 'head'), may hold values from -6 to 6
Outputs:
- attended: bfloat16 [2048, 6144], P('seq', 'head')
- grad_queries: bfloat16 [2048, 6144], P('seq', 'head')
- grad_keys: bfloat16 [2048, 6144], P('seq', 'head')
- grad_values: bfloat16 [2048, 6144], P('seq', 'head')
- grad_gain: float32 [6144], P('head')
The draws below stay inside these ranges and needn't reach their ends.
All inputs are finite; a program needn't handle non-finite values.
Results may differ from the reference program's by a relative error of at most 0.0058.
Values may be sent and summed in bfloat16 or wider, within the bound.
No kernel may reach another device: no remote copies, remote signals or barrier semaphores. Data moves between devices by JAX's collectives and lax.ppermute only.
A program may use at most 64 MiB of HBM per device.

```python
import jax
import jax.numpy as jnp
from jax import lax

HEADS = 48
HEAD_DIM = 128
TOK_DEV = 128
TOKENS = 2048


def block_scale(rng, shape, cuts, low, top_value):
    level, own = 1.0, jax.random.fold_in(rng, 6)
    for axis_at, blocks in cuts:
        heights = jnp.exp(jax.random.uniform(jax.random.fold_in(own, axis_at), (blocks,), jnp.float32, low / len(cuts), top_value / len(cuts)))
        level = level * jnp.repeat(heights, shape[axis_at] // blocks).reshape([-1 if axis == axis_at else 1 for axis in range(len(shape))])
    return level


def centred(stream_key, shape, scale, bound, pieces=(), kind=jnp.bfloat16):
    values = scale * jax.random.normal(stream_key, shape, jnp.float32)
    if pieces:
        values = values * block_scale(stream_key, shape, pieces, -0.22, 0.18)
    return jnp.clip(values, -bound, bound).astype(kind)


def setup_inputs(seed: int = 0) -> dict:
    seeds = jax.random.split(jax.random.key(seed), 6)
    return {
        "queries": centred(seeds[0], (TOKENS, HEADS * HEAD_DIM), 1.0, 6.0, ((0, 16), (1, 2))),
        "key_vectors": centred(seeds[1], (TOKENS, HEADS * HEAD_DIM), 1.0, 6.0, ((0, 16), (1, 2))),
        "value_vectors": centred(seeds[2], (TOKENS, HEADS * HEAD_DIM), 1.0, 6.0, ((0, 16), (1, 2))),
        "norm_gain": jnp.clip(1.0 + 0.18 * jax.random.normal(seeds[3], (HEADS * HEAD_DIM,), jnp.float32), 0.1, 1.9),
        "upstream": centred(seeds[4], (TOKENS, HEADS * HEAD_DIM), 1.0, 6.0, ((0, 16), (1, 2))),
    }


def reference(queries, key_vectors, value_vectors, norm_gain, upstream):
    blocks = TOKENS // TOK_DEV
    total_width = HEADS * HEAD_DIM
    shaped = (blocks, TOK_DEV, HEADS, HEAD_DIM)
    query_blocks = queries.reshape(shaped)
    key_blocks = key_vectors.reshape(shaped)
    value_blocks = value_vectors.reshape(shaped)
    upstream_blocks = upstream.reshape(shaped)
    gain_grid = norm_gain.astype(jnp.float32).reshape(HEADS, HEAD_DIM)
    positions = jnp.arange(TOK_DEV, dtype=jnp.int32)
    causal = (positions[None, :] <= positions[:, None])[None]

    def make_state(items):
        return jnp.einsum('thd,the->hde', items[0].astype(jnp.float32), items[1].astype(jnp.float32))
    local_state = lax.map(make_state, (key_blocks, value_blocks))
    running = jnp.cumsum(local_state, axis=0)
    prior = jnp.concatenate([jnp.zeros_like(local_state[:1]), running[:-1]], axis=0).astype(jnp.bfloat16)

    def make_weights(query_b, key_b):
        scores = jnp.einsum('thd,shd->hts', query_b.astype(jnp.float32), key_b.astype(jnp.float32))
        return jnp.where(causal, scores, 0.0).astype(jnp.bfloat16)

    def forward(items):
        query_b, key_b, value_b, prior_b, upstream_b = items
        weights = make_weights(query_b, key_b)
        out = jnp.einsum('hts,she->the', weights.astype(jnp.float32), value_b.astype(jnp.float32))
        out = out + jnp.einsum('thd,hde->the', query_b.astype(jnp.float32), prior_b.astype(jnp.float32))
        inv = lax.rsqrt(lax.optimization_barrier(jnp.sum(out * out, axis=(1, 2))) / total_width + 1e-06)[:, None, None]
        scaled = out * inv
        attended = (scaled * gain_grid).astype(jnp.bfloat16)
        grad_norm = upstream_b.astype(jnp.float32) * gain_grid
        mean_dot = (lax.optimization_barrier(jnp.sum(grad_norm * scaled, axis=(1, 2))) / total_width)[:, None, None]
        d_out = (inv * (grad_norm - scaled * mean_dot)).astype(jnp.bfloat16)
        gain_part = lax.optimization_barrier(jnp.sum(upstream_b.astype(jnp.float32) * scaled, axis=0))
        grad_state = jnp.einsum('thd,the->hde', query_b.astype(jnp.float32), d_out.astype(jnp.float32))
        return (attended, d_out, gain_part, grad_state)
    attended, d_out, gain_parts, grad_state = lax.map(forward, (query_blocks, key_blocks, value_blocks, prior, upstream_blocks))
    backwards = jnp.cumsum(grad_state[::-1], axis=0)[::-1]
    later = jnp.concatenate([backwards[1:], jnp.zeros_like(backwards[:1])], axis=0).astype(jnp.bfloat16)

    def backward(items):
        query_b, key_b, value_b, prior_b, later_b, d_out_b = items
        query_f = query_b.astype(jnp.float32)
        key_f = key_b.astype(jnp.float32)
        value_f = value_b.astype(jnp.float32)
        d_out_f = d_out_b.astype(jnp.float32)
        prior_f = prior_b.astype(jnp.float32)
        later_f = later_b.astype(jnp.float32)
        weights = make_weights(query_b, key_b).astype(jnp.float32)
        d_scores = jnp.where(causal, jnp.einsum('the,she->hts', d_out_f, value_f), 0.0)
        d_scores = d_scores.astype(jnp.bfloat16).astype(jnp.float32)
        grad_q = jnp.einsum('hts,shd->thd', d_scores, key_f) + jnp.einsum('the,hde->thd', d_out_f, prior_f)
        grad_k = jnp.einsum('hts,thd->shd', d_scores, query_f) + jnp.einsum('she,hde->shd', value_f, later_f)
        grad_v = jnp.einsum('hts,the->she', weights, d_out_f) + jnp.einsum('shd,hde->she', key_f, later_f)
        return (grad_q.astype(jnp.bfloat16), grad_k.astype(jnp.bfloat16), grad_v.astype(jnp.bfloat16))
    grad_q, grad_k, grad_v = lax.map(backward, (query_blocks, key_blocks, value_blocks, prior, later, d_out))
    flat = (TOKENS, total_width)
    return (attended.reshape(flat), grad_q.reshape(flat), grad_k.reshape(flat), grad_v.reshape(flat), lax.optimization_barrier(jnp.sum(gain_parts, axis=0)).reshape(total_width))
```

```python
import functools

import jax
import jax.numpy as jnp
from jax import lax
from jax.experimental import pallas as pl
from jax.experimental.pallas import tpu as pltpu
from jax.sharding import PartitionSpec as P

HEAD_DIM = 128
F32 = jnp.float32
BF16 = jnp.bfloat16
VMEM_LIMIT = 24 * 1024 * 1024


def call(kernel, out_shape, *args):
    whole = pl.BlockSpec(memory_space=pltpu.VMEM)
    return pl.pallas_call(
        kernel,
        out_shape=out_shape,
        in_specs=[whole] * len(args),
        out_specs=jax.tree.map(lambda _: whole, out_shape),
        compiler_params=pltpu.CompilerParams(vmem_limit_bytes=VMEM_LIMIT),
    )(*args)


def shape(dims, dtype):
    return jax.ShapeDtypeStruct(dims, dtype)


def dot(a, b, over):
    return lax.dot_general(a, b, ((over[:1], over[1:]), ((), ())), preferred_element_type=F32)


def split(value):
    high = value.astype(BF16)
    return high, (value - high.astype(F32)).astype(BF16)


def columns(head):
    return pl.ds(head * HEAD_DIM, HEAD_DIM)


def causal_mask(length):
    rows = lax.broadcasted_iota(jnp.int32, (length, length), 0)
    cols = lax.broadcasted_iota(jnp.int32, (length, length), 1)
    return cols <= rows


def state_kernel(heads, key_ref, value_ref, state_ref):
    for h in range(heads):
        part = dot(key_ref[:, columns(h)], value_ref[:, columns(h)], (0, 0))
        state_ref[columns(h), :] = part.astype(BF16)


def weights_kernel(heads, query_ref, key_ref, value_ref, weights_ref, inner_ref):
    mask = causal_mask(query_ref.shape[0])
    for h in range(heads):
        scores = dot(query_ref[:, columns(h)], key_ref[:, columns(h)], (1, 1))
        weights = jnp.where(mask, scores, 0.0).astype(BF16)
        weights_ref[h] = weights
        inner_ref[:, columns(h)] = dot(weights, value_ref[:, columns(h)], (1, 0))


def out_kernel(heads, query_ref, prior_ref, inner_ref, up_ref, gain_ref, out_ref, sums_ref):
    squares = jnp.zeros(sums_ref.shape[1:], F32)
    products = jnp.zeros(sums_ref.shape[1:], F32)
    for h in range(heads):
        out = inner_ref[:, columns(h)] + dot(query_ref[:, columns(h)], prior_ref[columns(h), :], (1, 0))
        out_ref[:, columns(h)] = out
        squares += out * out
        products += up_ref[:, columns(h)].astype(F32) * gain_ref[h][None] * out
    sums_ref[0] = squares
    sums_ref[1] = products


def token_factors(total_width, sums_refs):
    sums = functools.reduce(lambda a, b: a + b, [ref[...] for ref in sums_refs])
    inv = lax.rsqrt(jnp.sum(sums[0], axis=1, keepdims=True) / total_width + 1e-6)
    mean_dot = jnp.sum(sums[1], axis=1, keepdims=True) / total_width * inv
    return inv, mean_dot


def grad_out_kernel(heads, total_width, parts, *refs):
    out_ref, up_ref, gain_ref, query_ref, *sums_refs = refs[:-2]
    grad_ref, sent_ref = refs[-2:]
    inv, mean_dot = token_factors(total_width, sums_refs)
    rows = heads * HEAD_DIM // parts
    sent_ref[:, rows:, :] = jnp.zeros((parts, sent_ref.shape[1] - rows, HEAD_DIM), BF16)
    gains = []
    for h in range(heads):
        scaled = out_ref[:, columns(h)] * inv
        up = up_ref[:, columns(h)].astype(F32)
        grad = (inv * (up * gain_ref[h][None] - scaled * mean_dot)).astype(BF16)
        grad_ref[:, columns(h)] = grad
        state = dot(query_ref[:, columns(h)], grad, (0, 0)).astype(BF16)
        at = 0
        while at < HEAD_DIM:
            part, row = divmod(h * HEAD_DIM + at, rows)
            count = min(HEAD_DIM - at, rows - row)
            sent_ref[part, row:row + count, :] = state[at:at + count]
            at += count
        gains.append(jnp.sum(up * scaled, axis=0, keepdims=True))
    high, low = split(jnp.concatenate(gains, axis=0))
    for part in range(parts):
        sent_ref[part, rows:rows + heads, :] = high
        sent_ref[part, rows + heads:rows + 2 * heads, :] = low


def inner_grads_kernel(heads, total_width, *refs):
    (query_ref, key_ref, value_ref, gain_ref, out_ref, weights_ref, grad_ref, prior_ref,
     *sums_refs) = refs[:-4]
    attended_ref, grad_q_ref, inner_k_ref, inner_v_ref = refs[-4:]
    inv, _ = token_factors(total_width, sums_refs)
    mask = causal_mask(query_ref.shape[0])
    for h in range(heads):
        cols = columns(h)
        attended_ref[:, cols] = (out_ref[:, cols] * inv * gain_ref[h][None]).astype(BF16)
        grad = grad_ref[:, cols]
        scores = dot(grad, value_ref[:, cols], (1, 1))
        scores = jnp.where(mask, scores, 0.0).astype(BF16)
        grad_q = dot(scores, key_ref[:, cols], (1, 0)) + dot(grad, prior_ref[cols, :], (1, 1))
        grad_q_ref[:, cols] = grad_q.astype(BF16)
        inner_k_ref[:, cols] = dot(scores, query_ref[:, cols], (0, 0))
        inner_v_ref[:, cols] = dot(weights_ref[h], grad, (0, 0))


def last_grads_kernel(heads, key_ref, value_ref, later_ref, inner_k_ref, inner_v_ref, grad_k_ref, grad_v_ref):
    for h in range(heads):
        cols = columns(h)
        later = later_ref[cols, :]
        grad_k = inner_k_ref[:, cols] + dot(value_ref[:, cols], later, (1, 1))
        grad_k_ref[:, cols] = grad_k.astype(BF16)
        grad_v = inner_v_ref[:, cols] + dot(key_ref[:, cols], later, (1, 0))
        grad_v_ref[:, cols] = grad_v.astype(BF16)


def total_kernel(rows, heads, got_ref, total_ref):
    total = jnp.sum(got_ref[:, :rows, :].astype(F32), axis=0)
    total_ref[:rows, :] = total.astype(BF16)
    if heads:
        total_ref[rows:, :] = jnp.zeros((total_ref.shape[0] - rows, HEAD_DIM), BF16)
        high, low = split(gain_sum(rows, heads, got_ref))
        total_ref[rows:rows + heads, :] = high
        total_ref[rows + heads:rows + 2 * heads, :] = low


def gain_sum(rows, heads, ref):
    both = jnp.sum(ref[:, rows:rows + 2 * heads, :].astype(F32), axis=0)
    return both[:heads] + both[heads:]


def running_kernel(rows, heads, members, groups, reverse, *refs):
    outs = 2 if heads else 1
    got_ref, *total_refs = refs[:-outs]
    running_ref = refs[-outs]
    group = lax.axis_index("seq") // members
    state = jnp.zeros((rows, HEAD_DIM), F32)
    for step, ref in enumerate(total_refs, 1):
        ahead = group + step < groups if reverse else group >= step
        state += jnp.where(ahead, ref[:rows, :].astype(F32), 0.0)
    order = range(members - 1, -1, -1) if reverse else range(members)
    for member in order:
        running_ref[member] = state.astype(BF16)
        state += got_ref[member, :rows, :].astype(F32)
    if heads:
        gain = gain_sum(rows, heads, got_ref)
        for ref in total_refs:
            both = ref[rows:rows + 2 * heads, :].astype(F32)
            gain += both[:heads] + both[heads:]
        refs[-1][...] = gain


def exclusive_sums(shares, rows, heads, reverse):
    count = lax.axis_size("seq")
    members = shares.shape[0]
    groups = count // members
    index_groups = [list(range(g * members, (g + 1) * members)) for g in range(groups)]
    exchange = functools.partial(
        lax.all_to_all, axis_name="seq", split_axis=0, concat_axis=0, axis_index_groups=index_groups, tiled=True
    )
    got = exchange(shares)
    totals = []
    if groups > 1:
        total = call(
            functools.partial(total_kernel, rows, heads), shape(shares.shape[1:], BF16), got
        )
        for step in range(1, groups):
            hop = (-step if reverse else step) * members
            totals.append(lax.ppermute(total, "seq", [(i, (i + hop) % count) for i in range(count)]))
    outs = [shape((members, rows, HEAD_DIM), BF16)]
    if heads:
        outs.append(shape((heads, HEAD_DIM), F32))
    running, *gain = call(
        functools.partial(running_kernel, rows, heads, members, groups, reverse), outs, got, *totals
    )
    return exchange(running).reshape(members * rows, HEAD_DIM), *gain


def sums_over_heads(sums):
    count = lax.axis_size("head")
    return [sums] + [
        lax.ppermute(sums, "head", [(i, (i + step) % count) for i in range(count)])
        for step in range(1, count)
    ]


def group_size(count):
    members = 1
    while members < 8 and count % (2 * members) == 0:
        members *= 2
    return members


def body(queries, key_vectors, value_vectors, norm_gain, upstream):
    length, width = queries.shape
    heads = width // HEAD_DIM
    total_width = width * lax.axis_size("head")
    members = group_size(lax.axis_size("seq"))
    rows = width // members
    gain = norm_gain.reshape(heads, HEAD_DIM)
    flat16 = shape((length, width), BF16)
    flat32 = shape((length, width), F32)

    state = call(functools.partial(state_kernel, heads), shape((width, HEAD_DIM), BF16), key_vectors, value_vectors)
    (prior,) = exclusive_sums(state.reshape(members, rows, HEAD_DIM), rows, 0, False)
    weights, inner = call(
        functools.partial(weights_kernel, heads),
        [shape((heads, length, length), BF16), flat32],
        queries, key_vectors, value_vectors,
    )
    out, sums = call(
        functools.partial(out_kernel, heads),
        [flat32, shape((2, length, HEAD_DIM), F32)],
        queries, prior, inner, upstream, gain,
    )
    sums = sums_over_heads(sums)
    extra = -(-2 * heads // 16) * 16
    grad, shares = call(
        functools.partial(grad_out_kernel, heads, total_width, members),
        [flat16, shape((members, rows + extra, HEAD_DIM), BF16)],
        out, upstream, gain, queries, *sums,
    )
    later, grad_gain = exclusive_sums(shares, rows, heads, True)
    attended, grad_q, inner_k, inner_v = call(
        functools.partial(inner_grads_kernel, heads, total_width),
        [flat16, flat16, flat32, flat32],
        queries, key_vectors, value_vectors, gain, out, weights, grad, prior, *sums,
    )
    grad_k, grad_v = call(
        functools.partial(last_grads_kernel, heads),
        [flat16, flat16],
        key_vectors, value_vectors, later, inner_k, inner_v,
    )
    return attended, grad_q, grad_k, grad_v, grad_gain.reshape(-1)


def solution(mesh):
    split_both = P("seq", "head")
    in_specs = (split_both, split_both, split_both, P("head"), split_both)
    out_specs = (split_both, split_both, split_both, split_both, P("head"))
    return jax.shard_map(body, mesh=mesh, in_specs=in_specs, out_specs=out_specs, check_vma=False)
```

```python
import functools

import jax
import jax.numpy as jnp
from jax import lax
from jax.experimental import pallas as pl
from jax.experimental.pallas import tpu as pltpu
from jax.sharding import PartitionSpec as P

HEAD_DIM = 128
F32 = jnp.float32
BF16 = jnp.bfloat16
VMEM_LIMIT = 40 * 1024 * 1024
WHOLE = pl.BlockSpec(memory_space=pltpu.VMEM)
FAR = pl.BlockSpec(memory_space=pltpu.HBM)


def shape(dims, dtype):
    return jax.ShapeDtypeStruct(dims, dtype)


def call(kernel, out_shape, *args):
    return pl.pallas_call(
        kernel,
        out_shape=out_shape,
        in_specs=[WHOLE] * len(args),
        out_specs=jax.tree.map(lambda _: WHOLE, out_shape),
        compiler_params=pltpu.CompilerParams(vmem_limit_bytes=VMEM_LIMIT),
    )(*args)


def dot(a, b, over):
    return lax.dot_general(a, b, ((over[:1], over[1:]), ((), ())), preferred_element_type=F32)


def split(value):
    high = value.astype(BF16)
    return high, (value - high.astype(F32)).astype(BF16)


def columns(head):
    return pl.ds(head * HEAD_DIM, HEAD_DIM)


def causal_mask(length):
    rows = lax.broadcasted_iota(jnp.int32, (length, length), 0)
    cols = lax.broadcasted_iota(jnp.int32, (length, length), 1)
    return cols <= rows


def leaving(kernel, heads, ins, outs, near_outs=(), blocks=4):
    while heads % blocks:
        blocks -= 1
    step = heads // blocks
    count = len(outs)

    def whole(*refs):
        in_refs, refs = refs[:len(ins)], refs[len(ins):]
        out_refs, refs = refs[:count], refs[count:]
        near_refs, refs = refs[:len(near_outs)], refs[len(near_outs):]
        buffers, sems = refs[:count], refs[count]
        copies = []

        def done(h):
            if h % step == step - 1:
                span = pl.ds((h + 1 - step) * HEAD_DIM, step * HEAD_DIM)
                for i, (ref, buffer) in enumerate(zip(out_refs, buffers)):
                    copy = pltpu.make_async_copy(buffer.at[:, span], ref.at[:, span], sems.at[h // step, i])
                    copy.start()
                    copies.append(copy)

        kernel(done, *in_refs, *buffers, *near_refs)
        for copy in copies:
            copy.wait()

    return pl.pallas_call(
        whole,
        out_shape=list(outs) + list(near_outs),
        in_specs=[WHOLE] * len(ins),
        out_specs=[FAR] * count + [WHOLE] * len(near_outs),
        scratch_shapes=[pltpu.VMEM(a.shape, a.dtype) for a in outs] + [pltpu.SemaphoreType.DMA((blocks, count))],
        compiler_params=pltpu.CompilerParams(vmem_limit_bytes=VMEM_LIMIT),
    )(*ins)


def state_kernel(heads, key_ref, value_ref, state_ref):
    for h in range(heads):
        part = dot(key_ref[:, columns(h)], value_ref[:, columns(h)], (0, 0))
        state_ref[columns(h), :] = part.astype(BF16)


def weights_kernel(heads, query_ref, key_ref, value_ref, weights_ref, inner_ref):
    mask = causal_mask(query_ref.shape[0])
    for h in range(heads):
        scores = dot(query_ref[:, columns(h)], key_ref[:, columns(h)], (1, 1))
        weights = jnp.where(mask, scores, 0.0).astype(BF16)
        weights_ref[h] = weights
        inner_ref[:, columns(h)] = dot(weights, value_ref[:, columns(h)], (1, 0))


def out_kernel(heads, query_ref, inner_ref, up_ref, prior_ref, gain_ref, out_ref, sums_ref):
    squares = jnp.zeros(sums_ref.shape[1:], F32)
    products = jnp.zeros(sums_ref.shape[1:], F32)
    for h in range(heads):
        out = inner_ref[:, columns(h)] + dot(query_ref[:, columns(h)], prior_ref[columns(h), :], (1, 0))
        out_ref[:, columns(h)] = out
        squares += out * out
        products += up_ref[:, columns(h)].astype(F32) * gain_ref[h][None] * out
    sums_ref[0] = squares
    sums_ref[1] = products


def token_factors(total_width, sums_refs):
    sums = functools.reduce(lambda a, b: a + b, [ref[...] for ref in sums_refs])
    inv = lax.rsqrt(jnp.sum(sums[0], axis=1, keepdims=True) / total_width + 1e-6)
    mean_dot = jnp.sum(sums[1], axis=1, keepdims=True) / total_width * inv
    return inv, mean_dot


def gain_rows(heads, parts):
    return -(-heads // parts)


def grad_out_kernel(heads, total_width, parts, *refs):
    out_ref, up_ref, gain_ref, query_ref, *sums_refs = refs[:-2]
    grad_ref, sent_ref = refs[-2:]
    inv, mean_dot = token_factors(total_width, sums_refs)
    rows = heads * HEAD_DIM // parts
    each = gain_rows(heads, parts)
    sent_ref[:, rows:, :] = jnp.zeros((parts, sent_ref.shape[1] - rows, HEAD_DIM), BF16)
    gains = []
    for h in range(heads):
        scaled = out_ref[:, columns(h)] * inv
        up = up_ref[:, columns(h)].astype(F32)
        grad = (inv * (up * gain_ref[h][None] - scaled * mean_dot)).astype(BF16)
        grad_ref[:, columns(h)] = grad
        state = dot(query_ref[:, columns(h)], grad, (0, 0)).astype(BF16)
        at = 0
        while at < HEAD_DIM:
            part, row = divmod(h * HEAD_DIM + at, rows)
            count = min(HEAD_DIM - at, rows - row)
            sent_ref[part, row:row + count, :] = state[at:at + count]
            at += count
        gains.append(jnp.sum(up * scaled, axis=0, keepdims=True))
        if h % each == each - 1 or h == heads - 1:
            part = h // each
            high, low = split(jnp.concatenate(gains, axis=0))
            sent_ref[part, rows:rows + len(gains), :] = high
            sent_ref[part, rows + each:rows + each + len(gains), :] = low
            gains = []


def inner_grads_kernel(heads, total_width, done, *refs):
    (query_ref, key_ref, value_ref, out_ref, grad_ref, weights_ref, prior_ref, gain_ref, *sums_refs) = refs[:-4]
    attended_ref, grad_q_ref, inner_k_ref, inner_v_ref = refs[-4:]
    inv, _ = token_factors(total_width, sums_refs)
    mask = causal_mask(query_ref.shape[0])
    for h in range(heads):
        cols = columns(h)
        attended_ref[:, cols] = (out_ref[:, cols] * inv * gain_ref[h][None]).astype(BF16)
        grad = grad_ref[:, cols]
        scores = dot(grad, value_ref[:, cols], (1, 1))
        scores = jnp.where(mask, scores, 0.0).astype(BF16)
        grad_q = dot(scores, key_ref[:, cols], (1, 0)) + dot(grad, prior_ref[cols, :], (1, 1))
        grad_q_ref[:, cols] = grad_q.astype(BF16)
        inner_k_ref[:, cols] = dot(scores, query_ref[:, cols], (0, 0))
        inner_v_ref[:, cols] = dot(weights_ref[h], grad, (0, 0))
        done(h)


def last_grads_kernel(heads, parts, done, *refs):
    key_ref, value_ref, inner_k_ref, inner_v_ref, got_ref, grad_k_ref, grad_v_ref, gain_ref = refs
    rows = heads * HEAD_DIM // parts
    each = gain_rows(heads, parts)
    for h in range(heads):
        cols = columns(h)
        pieces, at = [], 0
        while at < HEAD_DIM:
            part, row = divmod(h * HEAD_DIM + at, rows)
            count = min(HEAD_DIM - at, rows - row)
            pieces.append(got_ref[part, row:row + count, :])
            at += count
        later = pieces[0] if len(pieces) == 1 else jnp.concatenate(pieces, axis=0)
        grad_k = inner_k_ref[:, cols] + dot(value_ref[:, cols], later, (1, 1))
        grad_k_ref[:, cols] = grad_k.astype(BF16)
        grad_v = inner_v_ref[:, cols] + dot(key_ref[:, cols], later, (1, 0))
        grad_v_ref[:, cols] = grad_v.astype(BF16)
        done(h)
        part, row = divmod(h, each)
        pair = got_ref[part, rows:rows + 2 * each, :].astype(F32)
        gain_ref[h:h + 1, :] = pair[row:row + 1] + pair[each + row:each + row + 1]


def gain_sum(rows, each, value):
    both = value[rows:rows + 2 * each, :]
    return both[:each] + both[each:]


def store_with_gain(ref, index, state, gain):
    rows, each = state.shape[0], gain.shape[0]
    high, low = split(gain)
    rest = jnp.zeros((ref.shape[-2] - rows - 2 * each, HEAD_DIM), F32)
    tail = jnp.concatenate([high.astype(F32), low.astype(F32), rest], axis=0).astype(BF16)
    ref[index + (slice(0, rows), slice(None))] = state.astype(BF16)
    ref[index + (slice(rows, None), slice(None))] = tail


def total_kernel(rows, each, got_ref, total_ref):
    total = jnp.sum(got_ref[...].astype(F32), axis=0)
    if each:
        store_with_gain(total_ref, (), total[:rows], gain_sum(rows, each, total))
    else:
        total_ref[...] = total.astype(BF16)


def running_kernel(rows, each, members, groups, reverse, *refs):
    got_ref, *total_refs, running_ref = refs
    group = lax.axis_index("seq") // members
    state = jnp.zeros((rows, HEAD_DIM), F32)
    for step, ref in enumerate(total_refs, 1):
        ahead = group + step < groups if reverse else group >= step
        state += jnp.where(ahead, ref[:rows, :].astype(F32), 0.0)
    if each:
        gain = gain_sum(rows, each, jnp.sum(got_ref[...].astype(F32), axis=0))
        for ref in total_refs:
            gain += gain_sum(rows, each, ref[...].astype(F32))
    order = range(members - 1, -1, -1) if reverse else range(members)
    for member in order:
        if each:
            store_with_gain(running_ref, (member,), state, gain)
        else:
            running_ref[member] = state.astype(BF16)
        state += got_ref[member, :rows, :].astype(F32)


def exclusive_sums(shares, rows, each, reverse, beside):
    count = lax.axis_size("seq")
    members = shares.shape[0]
    groups = count // members
    index_groups = [list(range(g * members, (g + 1) * members)) for g in range(groups)]
    exchange = functools.partial(
        lax.all_to_all, axis_name="seq", split_axis=0, concat_axis=0, axis_index_groups=index_groups, tiled=True
    )
    got = exchange(shares)
    totals = []
    if groups > 1:
        total = call(
            functools.partial(total_kernel, rows, each), shape(shares.shape[1:], BF16), got
        )
        for step in range(1, groups):
            hop = (-step if reverse else step) * members
            totals.append(lax.ppermute(total, "seq", [(i, (i + hop) % count) for i in range(count)]))
        got, work = beside(got, total)
    else:
        got, work = beside(got, got)
    running = call(
        functools.partial(running_kernel, rows, each, members, groups, reverse),
        shape(shares.shape, BF16), got, *totals,
    )
    return exchange(running), work


def sums_over_heads(sums):
    count = lax.axis_size("head")
    return [sums] + [
        lax.ppermute(sums, "head", [(i, (i + step) % count) for i in range(count)])
        for step in range(1, count)
    ]


def group_size(count):
    members = 1
    while members < 8 and count % (2 * members) == 0:
        members *= 2
    return members


def tied(value, after):
    return lax.optimization_barrier((value, after))[0]


def body(queries, key_vectors, value_vectors, norm_gain, upstream):
    length, width = queries.shape
    heads = width // HEAD_DIM
    total_width = width * lax.axis_size("head")
    members = group_size(lax.axis_size("seq"))
    rows = width // members
    gain = norm_gain.reshape(heads, HEAD_DIM)
    flat16 = shape((length, width), BF16)
    flat32 = shape((length, width), F32)

    state = call(functools.partial(state_kernel, heads), shape((width, HEAD_DIM), BF16), key_vectors, value_vectors)

    def inner_out(got, total):
        weights, inner = call(
            functools.partial(weights_kernel, heads),
            [shape((heads, length, length), BF16), flat32],
            tied(queries, total), key_vectors, value_vectors,
        )
        return tied(got, inner), (weights, inner)

    prior, (weights, inner) = exclusive_sums(state.reshape(members, rows, HEAD_DIM), rows, 0, False, inner_out)
    prior = prior.reshape(width, HEAD_DIM)
    out, sums = call(
        functools.partial(out_kernel, heads),
        [flat32, shape((2, length, HEAD_DIM), F32)],
        queries, inner, upstream, prior, gain,
    )
    sums = sums_over_heads(sums)
    each = gain_rows(heads, members)
    extra = -(-2 * each // 16) * 16
    grad, shares = call(
        functools.partial(grad_out_kernel, heads, total_width, members),
        [flat16, shape((members, rows + extra, HEAD_DIM), BF16)],
        out, upstream, gain, queries, *sums,
    )

    def inner_grads(got, total):
        attended, grad_q, inner_k, inner_v = leaving(
            functools.partial(inner_grads_kernel, heads, total_width), heads,
            [tied(queries, total), key_vectors, value_vectors, out, grad, weights, prior, gain, *sums],
            [flat16, flat16], [flat32, flat32],
        )
        return tied(got, inner_v), (attended, grad_q, inner_k, inner_v)

    later, (attended, grad_q, inner_k, inner_v) = exclusive_sums(shares, rows, each, True, inner_grads)
    grad_k, grad_v, grad_gain = leaving(
        functools.partial(last_grads_kernel, heads, members), heads,
        [key_vectors, value_vectors, inner_k, inner_v, later],
        [flat16, flat16], [shape((heads, HEAD_DIM), F32)],
    )
    return attended, grad_q, grad_k, grad_v, grad_gain.reshape(-1)


def solution(mesh):
    split_both = P("seq", "head")
    in_specs = (split_both, split_both, split_both, P("head"), split_both)
    out_specs = (split_both, split_both, split_both, split_both, P("head"))
    return jax.shard_map(body, mesh=mesh, in_specs=in_specs, out_specs=out_specs, check_vma=False)
```

```python
import functools

import jax
import jax.numpy as jnp
from jax import lax
from jax.experimental import pallas as pl
from jax.experimental.pallas import tpu as pltpu
from jax.sharding import PartitionSpec as P

HEAD_DIM = 128
F32 = jnp.float32
BF16 = jnp.bfloat16
VMEM_LIMIT = 40 * 1024 * 1024
WHOLE = pl.BlockSpec(memory_space=pltpu.VMEM)
FAR = pl.BlockSpec(memory_space=pltpu.HBM)


def shape(dims, dtype):
    return jax.ShapeDtypeStruct(dims, dtype)


def call(kernel, out_shape, *args):
    return pl.pallas_call(
        kernel,
        out_shape=out_shape,
        in_specs=[WHOLE] * len(args),
        out_specs=jax.tree.map(lambda _: WHOLE, out_shape),
        compiler_params=pltpu.CompilerParams(vmem_limit_bytes=VMEM_LIMIT),
    )(*args)


def dot(a, b, over):
    return lax.dot_general(a, b, ((over[:1], over[1:]), ((), ())), preferred_element_type=F32)


def split(value):
    high = value.astype(BF16)
    return high, (value - high.astype(F32)).astype(BF16)


def columns(head):
    return pl.ds(head * HEAD_DIM, HEAD_DIM)


def causal_mask(length):
    rows = lax.broadcasted_iota(jnp.int32, (length, length), 0)
    cols = lax.broadcasted_iota(jnp.int32, (length, length), 1)
    return cols <= rows


def first_core(mine, other):
    odd = lax.axis_index("head") % 2
    pl.when(odd == 0)(mine)
    pl.when(odd == 1)(other)


def leave(kernel, span, ins, outs, buffers, sems, blocks):
    if not span:
        return
    step = -(-len(span) // blocks)
    copies = []

    def done(h):
        place = h - span.start
        if place % step == step - 1 or h == span[-1]:
            first = span.start + place // step * step
            cols = pl.ds(first * HEAD_DIM, (h + 1 - first) * HEAD_DIM)
            for i, (out, buffer) in enumerate(zip(outs, buffers)):
                copy = pltpu.make_async_copy(buffer.at[:, cols], out.at[:, cols], sems.at[place // step, i])
                copy.start()
                copies.append(copy)

    kernel(span, done, *ins, *buffers)
    for copy in copies:
        copy.wait()


def leaving(kernel, spans, ins, outs, near_outs=(), held=(), blocks=4):
    count = len(outs)

    def whole(*refs):
        in_refs, refs = refs[:len(ins)], refs[len(ins) + len(held):]
        out_refs, refs = refs[:count], refs[count:]
        near_refs, refs = refs[:len(near_outs)], refs[len(near_outs):]
        buffers, sems = refs[:count], refs[count]
        work = lambda span: leave(kernel, span, in_refs + near_refs, out_refs, buffers, sems, blocks)
        if spans[0] == spans[1]:
            work(spans[0])
        else:
            first_core(lambda: work(spans[0]), lambda: work(spans[1]))

    return pl.pallas_call(
        whole,
        out_shape=list(outs) + list(near_outs),
        in_specs=[WHOLE] * len(ins) + [FAR] * len(held),
        out_specs=[FAR] * count + [WHOLE] * len(near_outs),
        scratch_shapes=[pltpu.VMEM(a.shape, a.dtype) for a in outs] + [pltpu.SemaphoreType.DMA((blocks, count))],
        input_output_aliases={len(ins) + i: i for i in range(len(held))},
        compiler_params=pltpu.CompilerParams(vmem_limit_bytes=VMEM_LIMIT),
    )(*ins, *held)


def inner_out_kernel(span, done, query_ref, key_ref, value_ref, weights_ref, inner_ref):
    mask = causal_mask(query_ref.shape[0])
    for h in span:
        cols = columns(h)
        scores = dot(query_ref[:, cols], key_ref[:, cols], (1, 1))
        weights = jnp.where(mask, scores, 0.0).astype(BF16)
        weights_ref[:, cols] = weights
        inner_ref[:, cols] = dot(weights, value_ref[:, cols], (1, 0))
        done(h)


def local_states(heads, early, queries, key_vectors, value_vectors, outs, blocks=2):
    length, width = key_vectors.shape
    while heads % blocks:
        blocks -= 1
    step = heads // blocks
    sources = [pltpu.with_memory_space_constraint(a, pltpu.HBM) for a in (key_vectors, value_vectors, queries)]

    def whole(*refs):
        far, (state_ref, *out_refs) = refs[:3], refs[3:6]
        key_ref, value_ref, query_ref, weights_ref, inner_ref, in_sems, out_sems = refs[6:]
        arrivals = []
        for block in range(blocks):
            cols = pl.ds(block * step * HEAD_DIM, step * HEAD_DIM)
            for i, (ref, buffer) in enumerate(((far[0], key_ref), (far[1], value_ref))):
                arrivals.append(pltpu.make_async_copy(ref.at[:, cols], buffer.at[:, cols], in_sems.at[i, block]))
        cols = pl.ds(0, max(len(early), 1) * HEAD_DIM)
        query_copy = pltpu.make_async_copy(far[2].at[:, cols], query_ref.at[:, cols], in_sems.at[2, 0])
        for copy in arrivals:
            copy.start()
        query_copy.start()
        for h in range(heads):
            if h % step == 0:
                for copy in arrivals[2 * (h // step):2 * (h // step) + 2]:
                    copy.wait()
            part = dot(key_ref[:, columns(h)], value_ref[:, columns(h)], (0, 0))
            state_ref[columns(h), :] = part.astype(BF16)
        query_copy.wait()
        ins = query_ref, key_ref, value_ref
        first_core(
            lambda: leave(inner_out_kernel, early, ins, out_refs, (weights_ref, inner_ref), out_sems, 1),
            lambda: None,
        )

    return pl.pallas_call(
        whole,
        out_shape=[shape((width, HEAD_DIM), BF16)] + outs,
        in_specs=[FAR] * 3,
        out_specs=[WHOLE, FAR, FAR],
        scratch_shapes=[pltpu.VMEM((length, width), BF16)] * 3 + [pltpu.VMEM(a.shape, a.dtype) for a in outs]
        + [pltpu.SemaphoreType.DMA((3, blocks)), pltpu.SemaphoreType.DMA((1, 2))],
        compiler_params=pltpu.CompilerParams(vmem_limit_bytes=VMEM_LIMIT),
    )(*sources)


def out_kernel(heads, query_ref, inner_ref, up_ref, prior_ref, gain_ref, out_ref, sums_ref):
    squares = jnp.zeros(sums_ref.shape[1:], F32)
    products = jnp.zeros(sums_ref.shape[1:], F32)
    for h in range(heads):
        out = inner_ref[:, columns(h)] + dot(query_ref[:, columns(h)], prior_ref[columns(h), :], (1, 0))
        out_ref[:, columns(h)] = out
        squares += out * out
        products += up_ref[:, columns(h)].astype(F32) * gain_ref[h][None] * out
    sums_ref[0] = squares
    sums_ref[1] = products


def token_factors(total_width, sums_refs):
    sums = functools.reduce(lambda a, b: a + b, [ref[...] for ref in sums_refs])
    inv = lax.rsqrt(jnp.sum(sums[0], axis=1, keepdims=True) / total_width + 1e-6)
    mean_dot = jnp.sum(sums[1], axis=1, keepdims=True) / total_width * inv
    return inv, mean_dot


def gain_rows(heads, parts):
    return -(-heads // parts)


def grad_out_kernel(heads, total_width, parts, *refs):
    out_ref, up_ref, gain_ref, query_ref, *sums_refs = refs[:-2]
    grad_ref, sent_ref = refs[-2:]
    inv, mean_dot = token_factors(total_width, sums_refs)
    rows = heads * HEAD_DIM // parts
    each = gain_rows(heads, parts)
    sent_ref[:, rows:, :] = jnp.zeros((parts, sent_ref.shape[1] - rows, HEAD_DIM), BF16)
    gains = []
    for h in range(heads):
        scaled = out_ref[:, columns(h)] * inv
        up = up_ref[:, columns(h)].astype(F32)
        grad = (inv * (up * gain_ref[h][None] - scaled * mean_dot)).astype(BF16)
        grad_ref[:, columns(h)] = grad
        state = dot(query_ref[:, columns(h)], grad, (0, 0)).astype(BF16)
        at = 0
        while at < HEAD_DIM:
            part, row = divmod(h * HEAD_DIM + at, rows)
            count = min(HEAD_DIM - at, rows - row)
            sent_ref[part, row:row + count, :] = state[at:at + count]
            at += count
        gains.append(jnp.sum(up * scaled, axis=0, keepdims=True))
        if h % each == each - 1 or h == heads - 1:
            part = h // each
            high, low = split(jnp.concatenate(gains, axis=0))
            sent_ref[part, rows:rows + len(gains), :] = high
            sent_ref[part, rows + each:rows + each + len(gains), :] = low
            gains = []


def inner_grads_kernel(span, done, *refs):
    query_ref, value_ref, grad_ref, weights_ref, scores_ref, inner_k_ref, inner_v_ref = refs
    mask = causal_mask(query_ref.shape[0])
    for h in span:
        cols = columns(h)
        grad = grad_ref[:, cols]
        scores = dot(grad, value_ref[:, cols], (1, 1))
        scores = jnp.where(mask, scores, 0.0).astype(BF16)
        scores_ref[:, cols] = scores
        inner_k_ref[:, cols] = dot(scores, query_ref[:, cols], (0, 0))
        inner_v_ref[:, cols] = dot(weights_ref[:, cols], grad, (0, 0))
        done(h)


def query_grads_kernel(total_width, span, done, *refs):
    scores_ref, key_ref, grad_ref, prior_ref, out_ref, gain_ref, *sums_refs = refs[:-2]
    attended_ref, grad_q_ref = refs[-2:]
    inv, _ = token_factors(total_width, sums_refs)
    for h in span:
        cols = columns(h)
        attended_ref[:, cols] = (out_ref[:, cols] * inv * gain_ref[h][None]).astype(BF16)
        grad_q = dot(scores_ref[:, cols], key_ref[:, cols], (1, 0)) + dot(grad_ref[:, cols], prior_ref[cols, :], (1, 1))
        grad_q_ref[:, cols] = grad_q.astype(BF16)
        done(h)


def last_grads_kernel(parts, span, done, *refs):
    key_ref, value_ref, inner_k_ref, inner_v_ref, got_ref, gain_ref, grad_k_ref, grad_v_ref = refs
    heads = len(span)
    rows = heads * HEAD_DIM // parts
    each = gain_rows(heads, parts)
    for h in span:
        cols = columns(h)
        pieces, at = [], 0
        while at < HEAD_DIM:
            part, row = divmod(h * HEAD_DIM + at, rows)
            count = min(HEAD_DIM - at, rows - row)
            pieces.append(got_ref[part, row:row + count, :])
            at += count
        later = pieces[0] if len(pieces) == 1 else jnp.concatenate(pieces, axis=0)
        grad_k = inner_k_ref[:, cols] + dot(value_ref[:, cols], later, (1, 1))
        grad_k_ref[:, cols] = grad_k.astype(BF16)
        grad_v = inner_v_ref[:, cols] + dot(key_ref[:, cols], later, (1, 0))
        grad_v_ref[:, cols] = grad_v.astype(BF16)
        done(h)
        part, row = divmod(h, each)
        pair = got_ref[part, rows:rows + 2 * each, :].astype(F32)
        gain_ref[h:h + 1, :] = pair[row:row + 1] + pair[each + row:each + row + 1]


def gain_sum(rows, each, value):
    both = value[rows:rows + 2 * each, :]
    return both[:each] + both[each:]


def store_with_gain(ref, index, state, gain):
    rows, each = state.shape[0], gain.shape[0]
    high, low = split(gain)
    rest = jnp.zeros((ref.shape[-2] - rows - 2 * each, HEAD_DIM), F32)
    tail = jnp.concatenate([high.astype(F32), low.astype(F32), rest], axis=0).astype(BF16)
    ref[index + (slice(0, rows), slice(None))] = state.astype(BF16)
    ref[index + (slice(rows, None), slice(None))] = tail


def total_kernel(rows, each, got_ref, total_ref):
    total = jnp.sum(got_ref[...].astype(F32), axis=0)
    if each:
        store_with_gain(total_ref, (), total[:rows], gain_sum(rows, each, total))
    else:
        total_ref[...] = total.astype(BF16)


def running_kernel(rows, each, members, groups, reverse, *refs):
    got_ref, *total_refs, running_ref = refs
    group = lax.axis_index("seq") // members
    state = jnp.zeros((rows, HEAD_DIM), F32)
    for step, ref in enumerate(total_refs, 1):
        ahead = group + step < groups if reverse else group >= step
        state += jnp.where(ahead, ref[:rows, :].astype(F32), 0.0)
    if each:
        gain = gain_sum(rows, each, jnp.sum(got_ref[...].astype(F32), axis=0))
        for ref in total_refs:
            gain += gain_sum(rows, each, ref[...].astype(F32))
    order = member_order(members)
    for block in range(members - 1, -1, -1) if reverse else range(members):
        member = order.index(block)
        if each:
            store_with_gain(running_ref, (member,), state, gain)
        else:
            running_ref[member] = state.astype(BF16)
        state += got_ref[member, :rows, :].astype(F32)


def member_order(members):
    quick = (3, 2, 6, 4, 1, 0, 7, 5)
    return list(quick if len(quick) == members else range(members))


def exclusive_sums(shares, rows, each, reverse, beside):
    count = lax.axis_size("seq")
    members = shares.shape[0]
    groups = count // members
    index_groups = [[g * members + block for block in member_order(members)] for g in range(groups)]
    exchange = functools.partial(
        lax.all_to_all, axis_name="seq", split_axis=0, concat_axis=0, axis_index_groups=index_groups, tiled=True
    )
    got = exchange(shares)
    totals = []
    if groups > 1:
        total = call(
            functools.partial(total_kernel, rows, each), shape(shares.shape[1:], BF16), got
        )
        for step in range(1, groups):
            hop = (-step if reverse else step) * members
            totals.append(lax.ppermute(total, "seq", [(i, (i + hop) % count) for i in range(count)]))
        got, work = beside(got, total)
    else:
        got, work = beside(got, got)
    running = call(
        functools.partial(running_kernel, rows, each, members, groups, reverse),
        shape(shares.shape, BF16), got, *totals,
    )
    return exchange(running), work


def sums_over_heads(sums):
    count = lax.axis_size("head")
    return [sums] + [
        lax.ppermute(sums, "head", [(i, (i + step) % count) for i in range(count)])
        for step in range(1, count)
    ]


def group_size(count):
    members = 1
    while members < 8 and count % (2 * members) == 0:
        members *= 2
    return members


def tied(value, after):
    return lax.optimization_barrier((value, after))[0]


def body(queries, key_vectors, value_vectors, norm_gain, upstream):
    length, width = queries.shape
    heads = width // HEAD_DIM
    total_width = width * lax.axis_size("head")
    members = group_size(lax.axis_size("seq"))
    rows = width // members
    gain = norm_gain.reshape(heads, HEAD_DIM)
    flat16 = shape((length, width), BF16)
    flat32 = shape((length, width), F32)
    flat_scores = shape((length, heads * length), BF16)

    every, none, early = range(heads), range(0), range(heads // 2)
    state, *held = local_states(heads, early, queries, key_vectors, value_vectors, [flat_scores, flat32])

    def inner_out(got, total):
        weights, inner = leaving(
            inner_out_kernel, (every[len(early):], every),
            [tied(queries, total), key_vectors, value_vectors], [flat_scores, flat32], (), held,
        )
        return tied(got, inner), (weights, inner)

    prior, (weights, inner) = exclusive_sums(state.reshape(members, rows, HEAD_DIM), rows, 0, False, inner_out)
    prior = prior.reshape(width, HEAD_DIM)
    out, sums = call(
        functools.partial(out_kernel, heads),
        [flat32, shape((2, length, HEAD_DIM), F32)],
        queries, inner, upstream, prior, gain,
    )
    sums = sums_over_heads(sums)
    each = gain_rows(heads, members)
    extra = -(-2 * each // 16) * 16
    grad, shares = call(
        functools.partial(grad_out_kernel, heads, total_width, members),
        [flat16, shape((members, rows + extra, HEAD_DIM), BF16)],
        out, upstream, gain, queries, *sums,
    )

    def inner_grads(spans, after, held=(), blocks=4):
        return leaving(
            inner_grads_kernel, spans, [tied(queries, after), value_vectors, grad, weights],
            [flat_scores, flat32, flat32], (), held, blocks,
        )

    def query_grads(spans, after, scores, held=(), blocks=4):
        return leaving(
            functools.partial(query_grads_kernel, total_width), spans,
            [scores, key_vectors, tied(grad, after), prior, out, gain, *sums], [flat16, flat16], (), held, blocks,
        )

    first = inner_grads((none, every), shares)
    ready = query_grads((none, every), first, first[0], (), 1)
    shares = tied(shares, ready)

    def grads_beside(got, total):
        late = inner_grads((every, none), total, first)
        results = query_grads((every, none), late, late[0], ready)
        return tied(got, results), (late, results)

    later, ((_, inner_k, inner_v), (attended, grad_q)) = exclusive_sums(shares, rows, each, True, grads_beside)
    grad_k, grad_v, grad_gain = leaving(
        functools.partial(last_grads_kernel, members), (every, every),
        [key_vectors, value_vectors, inner_k, inner_v, later],
        [flat16, flat16], [shape((heads, HEAD_DIM), F32)],
    )
    return attended, grad_q, grad_k, grad_v, grad_gain.reshape(-1)


def solution(mesh):
    split_both = P("seq", "head")
    in_specs = (split_both, split_both, split_both, P("head"), split_both)
    out_specs = (split_both, split_both, split_both, split_both, P("head"))
    return jax.shard_map(body, mesh=mesh, in_specs=in_specs, out_specs=out_specs, check_vma=False)
```

```python
import functools

import jax
import jax.numpy as jnp
from jax import lax
from jax.experimental import pallas as pl
from jax.experimental.pallas import tpu as pltpu
from jax.sharding import PartitionSpec as P

HEAD_DIM = 128
F32 = jnp.float32
BF16 = jnp.bfloat16
VMEM_LIMIT = 40 * 1024 * 1024
WHOLE = pl.BlockSpec(memory_space=pltpu.VMEM)
FAR = pl.BlockSpec(memory_space=pltpu.HBM)


def shape(dims, dtype):
    return jax.ShapeDtypeStruct(dims, dtype)


def call(kernel, out_shape, *args):
    return pl.pallas_call(
        kernel,
        out_shape=out_shape,
        in_specs=[WHOLE] * len(args),
        out_specs=jax.tree.map(lambda _: WHOLE, out_shape),
        compiler_params=pltpu.CompilerParams(vmem_limit_bytes=VMEM_LIMIT),
    )(*args)


def first_core(mine, other):
    odd = lax.axis_index("head") % 2
    pl.when(odd == 0)(mine)
    pl.when(odd == 1)(other)


def call_on(first, kernel, out_shape, *args):
    def whole(*refs):
        work, rest = lambda: kernel(*refs), lambda: None
        first_core(work if first else rest, rest if first else work)

    return call(whole, out_shape, *args)


def dot(a, b, over):
    return lax.dot_general(a, b, ((over[:1], over[1:]), ((), ())), preferred_element_type=F32)


def split(value):
    high = value.astype(BF16)
    return high, (value - high.astype(F32)).astype(BF16)


def columns(head):
    return pl.ds(head * HEAD_DIM, HEAD_DIM)


def causal_mask(length):
    rows = lax.broadcasted_iota(jnp.int32, (length, length), 0)
    cols = lax.broadcasted_iota(jnp.int32, (length, length), 1)
    return cols <= rows


def leave(kernel, span, ins, outs, buffers, sems, blocks):
    if not span:
        return
    step = -(-len(span) // blocks)
    copies = []

    def done(h):
        place = h - span.start
        if place % step == step - 1 or h == span[-1]:
            first = span.start + place // step * step
            cols = pl.ds(first * HEAD_DIM, (h + 1 - first) * HEAD_DIM)
            for i, (out, buffer) in enumerate(zip(outs, buffers)):
                copy = pltpu.make_async_copy(buffer.at[:, cols], out.at[:, cols], sems.at[place // step, i])
                copy.start()
                copies.append(copy)

    kernel(span, done, *ins, *buffers)
    for copy in copies:
        copy.wait()


def leaving(kernels, spans, ins, outs, near_outs=(), held=(), blocks=4):
    count = len(outs)

    def whole(*refs):
        in_refs, refs = refs[:len(ins)], refs[len(ins) + len(held):]
        out_refs, refs = refs[:count], refs[count:]
        near_refs, refs = refs[:len(near_outs)], refs[len(near_outs):]
        buffers, sems = refs[:count], refs[count]
        work = [
            functools.partial(leave, kernel, span, in_refs + near_refs, out_refs, buffers, sems, blocks)
            for kernel, span in zip(kernels, spans)
        ]
        first_core(*work)

    return pl.pallas_call(
        whole,
        out_shape=list(outs) + list(near_outs),
        in_specs=[WHOLE] * len(ins) + [FAR] * len(held),
        out_specs=[FAR] * count + [WHOLE] * len(near_outs),
        scratch_shapes=[pltpu.VMEM(a.shape, a.dtype) for a in outs] + [pltpu.SemaphoreType.DMA((blocks, count))],
        input_output_aliases={len(ins) + i: i for i in range(len(held))},
        compiler_params=pltpu.CompilerParams(vmem_limit_bytes=VMEM_LIMIT),
    )(*ins, *held)


def inner_out_kernel(heads, query_ref, key_ref, value_ref, weights_ref, inner_ref):
    mask = causal_mask(query_ref.shape[0])
    for h in range(heads):
        scores = dot(query_ref[:, columns(h)], key_ref[:, columns(h)], (1, 1))
        weights_ref[:, columns(h)] = jnp.where(mask, scores, 0.0).astype(BF16)
    for h in range(heads):
        inner_ref[:, columns(h)] = dot(weights_ref[:, columns(h)], value_ref[:, columns(h)], (1, 0))


def local_states(heads, queries, key_vectors, value_vectors, outs, blocks=2):
    length, width = key_vectors.shape
    while heads % blocks:
        blocks -= 1
    step = heads // blocks
    sources = [pltpu.with_memory_space_constraint(a, pltpu.HBM) for a in (key_vectors, value_vectors, queries)]

    def whole(*refs):
        far, (state_ref, *out_refs) = refs[:3], refs[3:6]
        key_ref, value_ref, query_ref, sems, query_sem = refs[6:]
        arrivals = []
        for block in range(blocks):
            cols = pl.ds(block * step * HEAD_DIM, step * HEAD_DIM)
            for i, (ref, buffer) in enumerate(((far[0], key_ref), (far[1], value_ref))):
                arrivals.append(pltpu.make_async_copy(ref.at[:, cols], buffer.at[:, cols], sems.at[i, block]))
        query_copy = pltpu.make_async_copy(far[2], query_ref, query_sem)
        for copy in arrivals:
            copy.start()
        first_core(query_copy.start, lambda: None)
        for h in range(heads):
            if h % step == 0:
                for copy in arrivals[2 * (h // step):2 * (h // step) + 2]:
                    copy.wait()
            part = dot(key_ref[:, columns(h)], value_ref[:, columns(h)], (0, 0))
            state_ref[columns(h), :] = part.astype(BF16)

        def early():
            query_copy.wait()
            inner_out_kernel(heads, query_ref, key_ref, value_ref, *out_refs)

        first_core(early, lambda: None)

    return pl.pallas_call(
        whole,
        out_shape=[shape((width, HEAD_DIM), BF16)] + outs,
        in_specs=[FAR] * 3,
        out_specs=[WHOLE] * 3,
        scratch_shapes=[pltpu.VMEM((length, width), BF16)] * 3
        + [pltpu.SemaphoreType.DMA((2, blocks)), pltpu.SemaphoreType.DMA],
        compiler_params=pltpu.CompilerParams(vmem_limit_bytes=VMEM_LIMIT),
    )(*sources)


def out_kernel(heads, query_ref, first_inner_ref, second_inner_ref, up_ref, prior_ref, gain_ref, out_ref, sums_ref):
    def work(inner_ref):
        squares = jnp.zeros(sums_ref.shape[1:], F32)
        products = jnp.zeros(sums_ref.shape[1:], F32)
        for h in range(heads):
            out = inner_ref[:, columns(h)] + dot(query_ref[:, columns(h)], prior_ref[columns(h), :], (1, 0))
            out_ref[:, columns(h)] = out
            squares += out * out
            products += up_ref[:, columns(h)].astype(F32) * gain_ref[h][None] * out
        sums_ref[0] = squares
        sums_ref[1] = products

    first_core(lambda: work(first_inner_ref), lambda: work(second_inner_ref))


def token_factors(total_width, sums_refs):
    sums = functools.reduce(lambda a, b: a + b, [ref[...] for ref in sums_refs])
    inv = lax.rsqrt(jnp.sum(sums[0], axis=1, keepdims=True) / total_width + 1e-6)
    mean_dot = jnp.sum(sums[1], axis=1, keepdims=True) / total_width * inv
    return inv, mean_dot


def gain_rows(heads, parts):
    return -(-heads // parts)


def grad_out_kernel(heads, total_width, parts, *refs):
    out_ref, up_ref, gain_ref, query_ref, *sums_refs = refs[:-2]
    grad_ref, sent_ref = refs[-2:]
    inv, mean_dot = token_factors(total_width, sums_refs)
    rows = heads * HEAD_DIM // parts
    each = gain_rows(heads, parts)
    sent_ref[:, rows:, :] = jnp.zeros((parts, sent_ref.shape[1] - rows, HEAD_DIM), BF16)
    gains = []
    for h in range(heads):
        scaled = out_ref[:, columns(h)] * inv
        up = up_ref[:, columns(h)].astype(F32)
        grad = (inv * (up * gain_ref[h][None] - scaled * mean_dot)).astype(BF16)
        grad_ref[:, columns(h)] = grad
        state = dot(query_ref[:, columns(h)], grad, (0, 0)).astype(BF16)
        at = 0
        while at < HEAD_DIM:
            part, row = divmod(h * HEAD_DIM + at, rows)
            count = min(HEAD_DIM - at, rows - row)
            sent_ref[part, row:row + count, :] = state[at:at + count]
            at += count
        gains.append(jnp.sum(up * scaled, axis=0, keepdims=True))
        if h % each == each - 1 or h == heads - 1:
            part = h // each
            high, low = split(jnp.concatenate(gains, axis=0))
            sent_ref[part, rows:rows + len(gains), :] = high
            sent_ref[part, rows + each:rows + each + len(gains), :] = low
            gains = []


def inner_grads_kernel(span, done, query_ref, value_ref, grad_ref, weights_ref, scores_ref, inner_k_ref, inner_v_ref):
    mask = causal_mask(query_ref.shape[0])
    for h in span:
        cols = columns(h)
        scores = dot(grad_ref[:, cols], value_ref[:, cols], (1, 1))
        scores_ref[:, cols] = jnp.where(mask, scores, 0.0).astype(BF16)
    for h in span:
        cols = columns(h)
        inner_k_ref[:, cols] = dot(scores_ref[:, cols], query_ref[:, cols], (0, 0))
        inner_v_ref[:, cols] = dot(weights_ref[:, cols], grad_ref[:, cols], (0, 0))
        done(h)


def query_grads_kernel(total_width, span, done, *refs):
    scores_ref, key_ref, grad_ref, prior_ref, out_ref, gain_ref, *sums_refs = refs[:-2]
    attended_ref, grad_q_ref = refs[-2:]
    inv, _ = token_factors(total_width, sums_refs)
    for h in span:
        cols = columns(h)
        attended_ref[:, cols] = (out_ref[:, cols] * inv * gain_ref[h][None]).astype(BF16)
        grad_q = dot(scores_ref[:, cols], key_ref[:, cols], (1, 0)) + dot(grad_ref[:, cols], prior_ref[cols, :], (1, 1))
        grad_q_ref[:, cols] = grad_q.astype(BF16)
        done(h)


def last_grads_kernel(parts, first, span, done, *refs):
    key_ref, value_ref, got_ref, *inner_refs, gain_ref, grad_k_ref, grad_v_ref = refs
    inner_k_ref, inner_v_ref = inner_refs[:2] if first else inner_refs[2:]
    heads = len(span)
    rows = heads * HEAD_DIM // parts
    each = gain_rows(heads, parts)
    for h in span:
        cols = columns(h)
        pieces, at = [], 0
        while at < HEAD_DIM:
            part, row = divmod(h * HEAD_DIM + at, rows)
            count = min(HEAD_DIM - at, rows - row)
            pieces.append(got_ref[part, row:row + count, :])
            at += count
        later = pieces[0] if len(pieces) == 1 else jnp.concatenate(pieces, axis=0)
        grad_k = inner_k_ref[:, cols] + dot(value_ref[:, cols], later, (1, 1))
        grad_k_ref[:, cols] = grad_k.astype(BF16)
        grad_v = inner_v_ref[:, cols] + dot(key_ref[:, cols], later, (1, 0))
        grad_v_ref[:, cols] = grad_v.astype(BF16)
        done(h)
        part, row = divmod(h, each)
        pair = got_ref[part, rows:rows + 2 * each, :].astype(F32)
        gain_ref[h:h + 1, :] = pair[row:row + 1] + pair[each + row:each + row + 1]


def gain_sum(rows, each, value):
    both = value[rows:rows + 2 * each, :]
    return both[:each] + both[each:]


def store_with_gain(ref, index, state, gain):
    rows, each = state.shape[0], gain.shape[0]
    high, low = split(gain)
    rest = jnp.zeros((ref.shape[-2] - rows - 2 * each, HEAD_DIM), F32)
    tail = jnp.concatenate([high.astype(F32), low.astype(F32), rest], axis=0).astype(BF16)
    ref[index + (slice(0, rows), slice(None))] = state.astype(BF16)
    ref[index + (slice(rows, None), slice(None))] = tail


def total_kernel(rows, each, got_ref, total_ref):
    total = jnp.sum(got_ref[...].astype(F32), axis=0)
    if each:
        store_with_gain(total_ref, (), total[:rows], gain_sum(rows, each, total))
    else:
        total_ref[...] = total.astype(BF16)


def running_kernel(rows, each, members, groups, reverse, *refs):
    got_ref, *total_refs, running_ref = refs
    group = lax.axis_index("seq") // members
    state = jnp.zeros((rows, HEAD_DIM), F32)
    for step, ref in enumerate(total_refs, 1):
        ahead = group + step < groups if reverse else group >= step
        state += jnp.where(ahead, ref[:rows, :].astype(F32), 0.0)
    if each:
        gain = gain_sum(rows, each, jnp.sum(got_ref[...].astype(F32), axis=0))
        for ref in total_refs:
            gain += gain_sum(rows, each, ref[...].astype(F32))
    order = member_order(members)
    for block in range(members - 1, -1, -1) if reverse else range(members):
        member = order.index(block)
        if each:
            store_with_gain(running_ref, (member,), state, gain)
        else:
            running_ref[member] = state.astype(BF16)
        state += got_ref[member, :rows, :].astype(F32)


def member_order(members):
    quick = (3, 2, 6, 4, 1, 0, 7, 5)
    return list(quick if len(quick) == members else range(members))


def exclusive_sums(shares, rows, each, reverse, beside):
    count = lax.axis_size("seq")
    members = shares.shape[0]
    groups = count // members
    index_groups = [[g * members + block for block in member_order(members)] for g in range(groups)]
    exchange = functools.partial(
        lax.all_to_all, axis_name="seq", split_axis=0, concat_axis=0, axis_index_groups=index_groups, tiled=True
    )
    got = exchange(shares)
    totals = []
    if groups > 1:
        total = call(
            functools.partial(total_kernel, rows, each), shape(shares.shape[1:], BF16), got
        )
        for step in range(1, groups):
            hop = (-step if reverse else step) * members
            totals.append(lax.ppermute(total, "seq", [(i, (i + hop) % count) for i in range(count)]))
        got, work = beside(got, total)
    else:
        got, work = beside(got, got)
    running = call(
        functools.partial(running_kernel, rows, each, members, groups, reverse),
        shape(shares.shape, BF16), got, *totals,
    )
    return exchange(running), work


def sums_over_heads(sums):
    count = lax.axis_size("head")
    return [sums] + [
        lax.ppermute(sums, "head", [(i, (i + step) % count) for i in range(count)])
        for step in range(1, count)
    ]


def group_size(count):
    members = 1
    while members < 8 and count % (2 * members) == 0:
        members *= 2
    return members


def tied(value, after):
    return lax.optimization_barrier((value, after))[0]


def body(queries, key_vectors, value_vectors, norm_gain, upstream):
    length, width = queries.shape
    heads = width // HEAD_DIM
    total_width = width * lax.axis_size("head")
    members = group_size(lax.axis_size("seq"))
    rows = width // members
    gain = norm_gain.reshape(heads, HEAD_DIM)
    flat16 = shape((length, width), BF16)
    flat32 = shape((length, width), F32)
    flat_scores = shape((length, heads * length), BF16)

    every, none = range(heads), range(0)
    inner_out = functools.partial(inner_out_kernel, heads)
    state, weights, inner = local_states(heads, queries, key_vectors, value_vectors, [flat_scores, flat32])

    def inner_out_beside(got, total):
        results = call_on(
            False, inner_out, [flat_scores, flat32], tied(queries, total), key_vectors, value_vectors
        )
        return tied(got, results), results

    prior, (second_weights, second_inner) = exclusive_sums(
        state.reshape(members, rows, HEAD_DIM), rows, 0, False, inner_out_beside
    )
    prior = prior.reshape(width, HEAD_DIM)
    out, sums = call(
        functools.partial(out_kernel, heads),
        [flat32, shape((2, length, HEAD_DIM), F32)],
        queries, inner, second_inner, upstream, prior, gain,
    )
    sums = sums_over_heads(sums)
    each = gain_rows(heads, members)
    extra = -(-2 * each // 16) * 16
    grad, shares = call(
        functools.partial(grad_out_kernel, heads, total_width, members),
        [flat16, shape((members, rows + extra, HEAD_DIM), BF16)],
        out, upstream, gain, queries, *sums,
    )

    inner_shapes = [flat_scores, flat32, flat32]

    def query_grads(spans, after, scores, held=(), blocks=4):
        return leaving(
            [functools.partial(query_grads_kernel, total_width)] * 2, spans,
            [scores, key_vectors, tied(grad, after), prior, out, gain, *sums], [flat16, flat16], (), held, blocks,
        )

    second_scores, *second_inner = leaving(
        [inner_grads_kernel] * 2, (none, every),
        [tied(queries, shares), value_vectors, grad, second_weights], inner_shapes, (), (), 8,
    )
    held = query_grads((none, every), second_inner, second_scores, (), 1)
    shares = tied(shares, held)

    def grads_beside(got, total):
        scores, *inner = call_on(
            True, functools.partial(inner_grads_kernel, every, lambda h: None), inner_shapes,
            tied(queries, total), value_vectors, grad, weights,
        )
        results = query_grads((every, none), inner, scores, held)
        return tied(got, results), (inner, results)

    later, (inner, (attended, grad_q)) = exclusive_sums(shares, rows, each, True, grads_beside)
    grad_k, grad_v, grad_gain = leaving(
        [functools.partial(last_grads_kernel, members, first) for first in (True, False)], (every, every),
        [key_vectors, value_vectors, later, *inner, *second_inner],
        [flat16, flat16], [shape((heads, HEAD_DIM), F32)],
    )
    return attended, grad_q, grad_k, grad_v, grad_gain.reshape(-1)


def solution(mesh):
    split_both = P("seq", "head")
    in_specs = (split_both, split_both, split_both, P("head"), split_both)
    out_specs = (split_both, split_both, split_both, split_both, P("head"))
    return jax.shard_map(body, mesh=mesh, in_specs=in_specs, out_specs=out_specs, check_vma=False)
```

```python
import functools

import jax
import jax.numpy as jnp
from jax import lax
from jax.experimental import pallas as pl
from jax.experimental.pallas import tpu as pltpu
from jax.sharding import PartitionSpec as P

HEAD_DIM = 128
F32 = jnp.float32
BF16 = jnp.bfloat16
VMEM_LIMIT = 40 * 1024 * 1024
WHOLE = pl.BlockSpec(memory_space=pltpu.VMEM)
FAR = pl.BlockSpec(memory_space=pltpu.HBM)


def shape(dims, dtype):
    return jax.ShapeDtypeStruct(dims, dtype)


def call(kernel, out_shape, *args):
    return pl.pallas_call(
        kernel,
        out_shape=out_shape,
        in_specs=[WHOLE] * len(args),
        out_specs=jax.tree.map(lambda _: WHOLE, out_shape),
        compiler_params=pltpu.CompilerParams(vmem_limit_bytes=VMEM_LIMIT),
    )(*args)


def first_core(mine, other):
    odd = lax.axis_index("head") % 2
    pl.when(odd == 0)(mine)
    pl.when(odd == 1)(other)


def call_on(first, kernel, out_shape, *args):
    def whole(*refs):
        work, rest = lambda: kernel(*refs), lambda: None
        first_core(work if first else rest, rest if first else work)

    return call(whole, out_shape, *args)


def dot(a, b, over):
    return lax.dot_general(a, b, ((over[:1], over[1:]), ((), ())), preferred_element_type=F32)


def split(value):
    high = value.astype(BF16)
    return high, (value - high.astype(F32)).astype(BF16)


def columns(head):
    return pl.ds(head * HEAD_DIM, HEAD_DIM)


def causal_mask(length):
    rows = lax.broadcasted_iota(jnp.int32, (length, length), 0)
    cols = lax.broadcasted_iota(jnp.int32, (length, length), 1)
    return cols <= rows


def leave(kernel, span, ins, outs, buffers, sems, blocks):
    if not span:
        return
    step = -(-len(span) // blocks)
    copies = []

    def done(h):
        place = h - span.start
        if place % step == step - 1 or h == span[-1]:
            first = span.start + place // step * step
            cols = pl.ds(first * HEAD_DIM, (h + 1 - first) * HEAD_DIM)
            for i, (out, buffer) in enumerate(zip(outs, buffers)):
                copy = pltpu.make_async_copy(buffer.at[:, cols], out.at[:, cols], sems.at[place // step, i])
                copy.start()
                copies.append(copy)

    kernel(span, done, *ins, *buffers)
    for copy in copies:
        copy.wait()


def leaving(kernels, spans, ins, outs, near_outs=(), held=(), blocks=4):
    count = len(outs)

    def whole(*refs):
        in_refs, refs = refs[:len(ins)], refs[len(ins) + len(held):]
        out_refs, refs = refs[:count], refs[count:]
        near_refs, refs = refs[:len(near_outs)], refs[len(near_outs):]
        buffers, sems = refs[:count], refs[count]
        work = [
            functools.partial(leave, kernel, span, in_refs + near_refs, out_refs, buffers, sems, blocks)
            for kernel, span in zip(kernels, spans)
        ]
        first_core(*work)

    return pl.pallas_call(
        whole,
        out_shape=list(outs) + list(near_outs),
        in_specs=[WHOLE] * len(ins) + [FAR] * len(held),
        out_specs=[FAR] * count + [WHOLE] * len(near_outs),
        scratch_shapes=[pltpu.VMEM(a.shape, a.dtype) for a in outs] + [pltpu.SemaphoreType.DMA((blocks, count))],
        input_output_aliases={len(ins) + i: i for i in range(len(held))},
        compiler_params=pltpu.CompilerParams(vmem_limit_bytes=VMEM_LIMIT),
    )(*ins, *held)


def inner_out_kernel(heads, query_ref, key_ref, value_ref, weights_ref, inner_ref):
    mask = causal_mask(query_ref.shape[0])
    for h in range(heads):
        scores = dot(query_ref[:, columns(h)], key_ref[:, columns(h)], (1, 1))
        weights_ref[:, columns(h)] = jnp.where(mask, scores, 0.0).astype(BF16)
    for h in range(heads):
        inner_ref[:, columns(h)] = dot(weights_ref[:, columns(h)], value_ref[:, columns(h)], (1, 0))


def local_states(heads, queries, key_vectors, value_vectors, outs, blocks=2):
    length, width = key_vectors.shape
    while heads % blocks:
        blocks -= 1
    step = heads // blocks
    sources = [pltpu.with_memory_space_constraint(a, pltpu.HBM) for a in (key_vectors, value_vectors, queries)]

    def whole(*refs):
        far, (state_ref, *out_refs) = refs[:3], refs[3:6]
        key_ref, value_ref, query_ref, sems, query_sem = refs[6:]
        arrivals = []
        for block in range(blocks):
            cols = pl.ds(block * step * HEAD_DIM, step * HEAD_DIM)
            for i, (ref, buffer) in enumerate(((far[0], key_ref), (far[1], value_ref))):
                arrivals.append(pltpu.make_async_copy(ref.at[:, cols], buffer.at[:, cols], sems.at[i, block]))
        query_copy = pltpu.make_async_copy(far[2], query_ref, query_sem)
        for copy in arrivals:
            copy.start()
        first_core(query_copy.start, lambda: None)
        for h in range(heads):
            if h % step == 0:
                for copy in arrivals[2 * (h // step):2 * (h // step) + 2]:
                    copy.wait()
            part = dot(key_ref[:, columns(h)], value_ref[:, columns(h)], (0, 0))
            state_ref[columns(h), :] = part.astype(BF16)

        def early():
            query_copy.wait()
            inner_out_kernel(heads, query_ref, key_ref, value_ref, *out_refs)

        first_core(early, lambda: None)

    return pl.pallas_call(
        whole,
        out_shape=[shape((width, HEAD_DIM), BF16)] + outs,
        in_specs=[FAR] * 3,
        out_specs=[WHOLE] * 3,
        scratch_shapes=[pltpu.VMEM((length, width), BF16)] * 3
        + [pltpu.SemaphoreType.DMA((2, blocks)), pltpu.SemaphoreType.DMA],
        compiler_params=pltpu.CompilerParams(vmem_limit_bytes=VMEM_LIMIT),
    )(*sources)


def out_kernel(heads, query_ref, first_inner_ref, second_inner_ref, up_ref, prior_ref, gain_ref, out_ref, sums_ref):
    def work(inner_ref):
        squares = jnp.zeros(sums_ref.shape[1:], F32)
        products = jnp.zeros(sums_ref.shape[1:], F32)
        for h in range(heads):
            out = inner_ref[:, columns(h)] + dot(query_ref[:, columns(h)], prior_ref[columns(h), :], (1, 0))
            out_ref[:, columns(h)] = out
            squares += out * out
            products += up_ref[:, columns(h)].astype(F32) * gain_ref[h][None] * out
        sums_ref[0] = squares
        sums_ref[1] = products

    first_core(lambda: work(first_inner_ref), lambda: work(second_inner_ref))


def token_factors(total_width, sums_refs):
    sums = functools.reduce(lambda a, b: a + b, [ref[...] for ref in sums_refs])
    inv = lax.rsqrt(jnp.sum(sums[0], axis=1, keepdims=True) / total_width + 1e-6)
    mean_dot = jnp.sum(sums[1], axis=1, keepdims=True) / total_width * inv
    return inv, mean_dot


def gain_rows(heads, parts):
    return -(-heads // parts)


def grad_out_kernel(heads, total_width, parts, *refs):
    out_ref, up_ref, gain_ref, query_ref, *sums_refs = refs[:-2]
    grad_ref, sent_ref = refs[-2:]
    inv, mean_dot = token_factors(total_width, sums_refs)
    rows = heads * HEAD_DIM // parts
    each = gain_rows(heads, parts)
    sent_ref[:, rows:, :] = jnp.zeros((parts, sent_ref.shape[1] - rows, HEAD_DIM), BF16)
    gains = []
    for h in range(heads):
        scaled = out_ref[:, columns(h)] * inv
        up = up_ref[:, columns(h)].astype(F32)
        grad = (inv * (up * gain_ref[h][None] - scaled * mean_dot)).astype(BF16)
        grad_ref[:, columns(h)] = grad
        state = dot(query_ref[:, columns(h)], grad, (0, 0)).astype(BF16)
        at = 0
        while at < HEAD_DIM:
            part, row = divmod(h * HEAD_DIM + at, rows)
            count = min(HEAD_DIM - at, rows - row)
            sent_ref[part, row:row + count, :] = state[at:at + count]
            at += count
        gains.append(jnp.sum(up * scaled, axis=0, keepdims=True))
        if h % each == each - 1 or h == heads - 1:
            part = h // each
            high, low = split(jnp.concatenate(gains, axis=0))
            sent_ref[part, rows:rows + len(gains), :] = high
            sent_ref[part, rows + each:rows + each + len(gains), :] = low
            gains = []


def inner_grads_kernel(span, done, query_ref, value_ref, grad_ref, weights_ref, scores_ref, inner_k_ref, inner_v_ref):
    mask = causal_mask(query_ref.shape[0])
    for h in span:
        cols = columns(h)
        scores = dot(grad_ref[:, cols], value_ref[:, cols], (1, 1))
        scores_ref[:, cols] = jnp.where(mask, scores, 0.0).astype(BF16)
    for h in span:
        cols = columns(h)
        inner_k_ref[:, cols] = dot(scores_ref[:, cols], query_ref[:, cols], (0, 0))
        inner_v_ref[:, cols] = dot(weights_ref[:, cols], grad_ref[:, cols], (0, 0))
        done(h)


def query_grads_kernel(total_width, span, done, *refs):
    scores_ref, key_ref, grad_ref, prior_ref, out_ref, gain_ref, *sums_refs = refs[:-2]
    attended_ref, grad_q_ref = refs[-2:]
    inv, _ = token_factors(total_width, sums_refs)
    for h in span:
        cols = columns(h)
        attended_ref[:, cols] = (out_ref[:, cols] * inv * gain_ref[h][None]).astype(BF16)
        grad_q = dot(scores_ref[:, cols], key_ref[:, cols], (1, 0)) + dot(grad_ref[:, cols], prior_ref[cols, :], (1, 1))
        grad_q_ref[:, cols] = grad_q.astype(BF16)
        done(h)


def last_grads_kernel(parts, first, span, done, *refs):
    key_ref, value_ref, got_ref, *inner_refs, gain_ref, grad_k_ref, grad_v_ref = refs
    inner_k_ref, inner_v_ref = inner_refs[:2] if first else inner_refs[2:]
    heads = len(span)
    rows = heads * HEAD_DIM // parts
    each = gain_rows(heads, parts)
    for h in span:
        cols = columns(h)
        pieces, at = [], 0
        while at < HEAD_DIM:
            part, row = divmod(h * HEAD_DIM + at, rows)
            count = min(HEAD_DIM - at, rows - row)
            pieces.append(got_ref[part, row:row + count, :])
            at += count
        later = pieces[0] if len(pieces) == 1 else jnp.concatenate(pieces, axis=0)
        grad_k = inner_k_ref[:, cols] + dot(value_ref[:, cols], later, (1, 1))
        grad_k_ref[:, cols] = grad_k.astype(BF16)
        grad_v = inner_v_ref[:, cols] + dot(key_ref[:, cols], later, (1, 0))
        grad_v_ref[:, cols] = grad_v.astype(BF16)
        done(h)
    for part in range(-(-heads // each)):
        pair = got_ref[part, rows:rows + 2 * each, :].astype(F32)
        own = min(each, heads - part * each)
        gain_ref[part * each:part * each + own, :] = pair[:own] + pair[each:each + own]


def gain_sum(rows, each, value):
    both = value[rows:rows + 2 * each, :]
    return both[:each] + both[each:]


def store_with_gain(ref, index, state, gain):
    rows, each = state.shape[0], gain.shape[0]
    high, low = split(gain)
    rest = jnp.zeros((ref.shape[-2] - rows - 2 * each, HEAD_DIM), F32)
    tail = jnp.concatenate([high.astype(F32), low.astype(F32), rest], axis=0).astype(BF16)
    ref[index + (slice(0, rows), slice(None))] = state.astype(BF16)
    ref[index + (slice(rows, None), slice(None))] = tail


def total_kernel(rows, each, got_ref, total_ref):
    total = jnp.sum(got_ref[...].astype(F32), axis=0)
    if each:
        store_with_gain(total_ref, (), total[:rows], gain_sum(rows, each, total))
    else:
        total_ref[...] = total.astype(BF16)


def running_kernel(rows, each, members, groups, reverse, *refs):
    got_ref, *total_refs, running_ref = refs
    group = lax.axis_index("seq") // members
    state = jnp.zeros((rows, HEAD_DIM), F32)
    for step, ref in enumerate(total_refs, 1):
        ahead = group + step < groups if reverse else group >= step
        state += jnp.where(ahead, ref[:rows, :].astype(F32), 0.0)
    if each:
        gain = gain_sum(rows, each, jnp.sum(got_ref[...].astype(F32), axis=0))
        for ref in total_refs:
            gain += gain_sum(rows, each, ref[...].astype(F32))
    order = member_order(members)
    for block in range(members - 1, -1, -1) if reverse else range(members):
        member = order.index(block)
        if each:
            store_with_gain(running_ref, (member,), state, gain)
        else:
            running_ref[member] = state.astype(BF16)
        state += got_ref[member, :rows, :].astype(F32)


def member_order(members):
    quick = (3, 1, 5, 6, 7, 4, 0, 2)
    return list(quick if len(quick) == members else range(members))


def exclusive_sums(shares, rows, each, reverse, beside):
    count = lax.axis_size("seq")
    members = shares.shape[0]
    groups = count // members
    index_groups = [[g * members + block for block in member_order(members)] for g in range(groups)]
    exchange = functools.partial(
        lax.all_to_all, axis_name="seq", split_axis=0, concat_axis=0, axis_index_groups=index_groups, tiled=True
    )
    got = exchange(shares)
    totals = []
    if groups > 1:
        total = call(
            functools.partial(total_kernel, rows, each), shape(shares.shape[1:], BF16), got
        )
        for step in range(1, groups):
            hop = (-step if reverse else step) * members
            totals.append(lax.ppermute(total, "seq", [(i, (i + hop) % count) for i in range(count)]))
        got, work = beside(got, total)
    else:
        got, work = beside(got, got)
    running = call(
        functools.partial(running_kernel, rows, each, members, groups, reverse),
        shape(shares.shape, BF16), got, *totals,
    )
    return exchange(running), work


def sums_over_heads(sums):
    count = lax.axis_size("head")
    return [sums] + [
        lax.ppermute(sums, "head", [(i, (i + step) % count) for i in range(count)])
        for step in range(1, count)
    ]


def group_size(count):
    members = 1
    while members < 8 and count % (2 * members) == 0:
        members *= 2
    return members


def tied(value, after):
    return lax.optimization_barrier((value, after))[0]


def body(queries, key_vectors, value_vectors, norm_gain, upstream):
    length, width = queries.shape
    heads = width // HEAD_DIM
    total_width = width * lax.axis_size("head")
    members = group_size(lax.axis_size("seq"))
    rows = width // members
    gain = norm_gain.reshape(heads, HEAD_DIM)
    flat16 = shape((length, width), BF16)
    flat32 = shape((length, width), F32)
    flat_scores = shape((length, heads * length), BF16)

    every, none = range(heads), range(0)
    inner_out = functools.partial(inner_out_kernel, heads)
    state, weights, inner = local_states(heads, queries, key_vectors, value_vectors, [flat_scores, flat32])

    def inner_out_beside(got, total):
        results = call_on(
            False, inner_out, [flat_scores, flat32], tied(queries, total), key_vectors, value_vectors
        )
        return tied(got, results), results

    prior, (second_weights, second_inner) = exclusive_sums(
        state.reshape(members, rows, HEAD_DIM), rows, 0, False, inner_out_beside
    )
    prior = prior.reshape(width, HEAD_DIM)
    out, sums = call(
        functools.partial(out_kernel, heads),
        [flat32, shape((2, length, HEAD_DIM), F32)],
        queries, inner, second_inner, upstream, prior, gain,
    )
    sums = sums_over_heads(sums)
    each = gain_rows(heads, members)
    extra = -(-2 * each // 16) * 16
    grad, shares = call(
        functools.partial(grad_out_kernel, heads, total_width, members),
        [flat16, shape((members, rows + extra, HEAD_DIM), BF16)],
        out, upstream, gain, queries, *sums,
    )

    inner_shapes = [flat_scores, flat32, flat32]

    def query_grads(spans, after, scores, held=(), blocks=4):
        return leaving(
            [functools.partial(query_grads_kernel, total_width)] * 2, spans,
            [scores, key_vectors, tied(grad, after), prior, out, gain, *sums], [flat16, flat16], (), held, blocks,
        )

    second_scores, *second_inner = leaving(
        [inner_grads_kernel] * 2, (none, every),
        [tied(queries, shares), value_vectors, grad, second_weights], inner_shapes, (), (), 8,
    )
    held = query_grads((none, every), second_inner, second_scores, (), 1)
    shares = tied(shares, held)

    def grads_beside(got, total):
        scores, *inner = call_on(
            True, functools.partial(inner_grads_kernel, every, lambda h: None), inner_shapes,
            tied(queries, total), value_vectors, grad, weights,
        )
        results = query_grads((every, none), inner, scores, held)
        return tied(got, results), (inner, results)

    later, (inner, (attended, grad_q)) = exclusive_sums(shares, rows, each, True, grads_beside)
    grad_k, grad_v, grad_gain = leaving(
        [functools.partial(last_grads_kernel, members, first) for first in (True, False)], (every, every),
        [key_vectors, value_vectors, later, *inner, *second_inner],
        [flat16, flat16], [shape((heads, HEAD_DIM), F32)], (), 6
    )
    return attended, grad_q, grad_k, grad_v, grad_gain.reshape(-1)


def solution(mesh):
    split_both = P("seq", "head")
    in_specs = (split_both, split_both, split_both, P("head"), split_both)
    out_specs = (split_both, split_both, split_both, split_both, P("head"))
    return jax.shard_map(body, mesh=mesh, in_specs=in_specs, out_specs=out_specs, check_vma=False)
```

```python
import functools

import jax
import jax.numpy as jnp
from jax import lax
from jax.experimental import pallas as pl
from jax.experimental.pallas import tpu as pltpu
from jax.sharding import PartitionSpec as P

HEAD_DIM = 128
F32 = jnp.float32
BF16 = jnp.bfloat16
VMEM_LIMIT = 40 * 1024 * 1024
WHOLE = pl.BlockSpec(memory_space=pltpu.VMEM)
FAR = pl.BlockSpec(memory_space=pltpu.HBM)


def shape(dims, dtype):
    return jax.ShapeDtypeStruct(dims, dtype)


def call(kernel, out_shape, *args):
    return pl.pallas_call(
        kernel,
        out_shape=out_shape,
        in_specs=[WHOLE] * len(args),
        out_specs=jax.tree.map(lambda _: WHOLE, out_shape),
        compiler_params=pltpu.CompilerParams(vmem_limit_bytes=VMEM_LIMIT),
    )(*args)


def first_core(mine, other):
    odd = lax.axis_index("head") % 2
    pl.when(odd == 0)(mine)
    pl.when(odd == 1)(other)


def call_on(first, kernel, out_shape, *args):
    def whole(*refs):
        work, rest = lambda: kernel(*refs), lambda: None
        first_core(work if first else rest, rest if first else work)

    return call(whole, out_shape, *args)


def dot(a, b, over):
    return lax.dot_general(a, b, ((over[:1], over[1:]), ((), ())), preferred_element_type=F32)


def split(value):
    high = value.astype(BF16)
    return high, (value - high.astype(F32)).astype(BF16)


def columns(head):
    return pl.ds(head * HEAD_DIM, HEAD_DIM)


def causal_mask(length):
    rows = lax.broadcasted_iota(jnp.int32, (length, length), 0)
    cols = lax.broadcasted_iota(jnp.int32, (length, length), 1)
    return cols <= rows


def leave(kernel, span, ins, outs, buffers, sems, blocks):
    if not span:
        return
    step = -(-len(span) // blocks)
    copies = []

    def done(h):
        place = h - span.start
        if place % step == step - 1 or h == span[-1]:
            first = span.start + place // step * step
            cols = pl.ds(first * HEAD_DIM, (h + 1 - first) * HEAD_DIM)
            for i, (out, buffer) in enumerate(zip(outs, buffers)):
                copy = pltpu.make_async_copy(buffer.at[:, cols], out.at[:, cols], sems.at[place // step, i])
                copy.start()
                copies.append(copy)

    kernel(span, done, *ins, *buffers)
    for copy in copies:
        copy.wait()


def leaving(kernels, spans, ins, outs, near_outs=(), held=(), blocks=4):
    count = len(outs)

    def whole(*refs):
        in_refs, refs = refs[:len(ins)], refs[len(ins) + len(held):]
        out_refs, refs = refs[:count], refs[count:]
        near_refs, refs = refs[:len(near_outs)], refs[len(near_outs):]
        buffers, sems = refs[:count], refs[count]
        work = [
            functools.partial(leave, kernel, span, in_refs + near_refs, out_refs, buffers, sems, blocks)
            for kernel, span in zip(kernels, spans)
        ]
        first_core(*work)

    return pl.pallas_call(
        whole,
        out_shape=list(outs) + list(near_outs),
        in_specs=[WHOLE] * len(ins) + [FAR] * len(held),
        out_specs=[FAR] * count + [WHOLE] * len(near_outs),
        scratch_shapes=[pltpu.VMEM(a.shape, a.dtype) for a in outs] + [pltpu.SemaphoreType.DMA((blocks, count))],
        input_output_aliases={len(ins) + i: i for i in range(len(held))},
        compiler_params=pltpu.CompilerParams(vmem_limit_bytes=VMEM_LIMIT),
    )(*ins, *held)


def inner_out_kernel(heads, query_ref, key_ref, value_ref, weights_ref, inner_ref):
    mask = causal_mask(query_ref.shape[0])
    for h in range(heads):
        scores = dot(query_ref[:, columns(h)], key_ref[:, columns(h)], (1, 1))
        weights_ref[:, columns(h)] = jnp.where(mask, scores, 0.0).astype(BF16)
    for h in range(heads):
        inner_ref[:, columns(h)] = dot(weights_ref[:, columns(h)], value_ref[:, columns(h)], (1, 0))


def local_states(heads, queries, key_vectors, value_vectors, outs, blocks=2):
    length, width = key_vectors.shape
    while heads % blocks:
        blocks -= 1
    step = heads // blocks
    sources = [pltpu.with_memory_space_constraint(a, pltpu.HBM) for a in (key_vectors, value_vectors, queries)]

    def whole(*refs):
        far, (state_ref, *out_refs) = refs[:3], refs[3:6]
        key_ref, value_ref, query_ref, sems, query_sem = refs[6:]
        arrivals = []
        for block in range(blocks):
            cols = pl.ds(block * step * HEAD_DIM, step * HEAD_DIM)
            for i, (ref, buffer) in enumerate(((far[0], key_ref), (far[1], value_ref))):
                arrivals.append(pltpu.make_async_copy(ref.at[:, cols], buffer.at[:, cols], sems.at[i, block]))
        query_copy = pltpu.make_async_copy(far[2], query_ref, query_sem)
        for copy in arrivals:
            copy.start()
        first_core(query_copy.start, lambda: None)
        for h in range(heads):
            if h % step == 0:
                for copy in arrivals[2 * (h // step):2 * (h // step) + 2]:
                    copy.wait()
            part = dot(key_ref[:, columns(h)], value_ref[:, columns(h)], (0, 0))
            state_ref[columns(h), :] = part.astype(BF16)

        def early():
            query_copy.wait()
            inner_out_kernel(heads, query_ref, key_ref, value_ref, *out_refs)

        first_core(early, lambda: None)

    return pl.pallas_call(
        whole,
        out_shape=[shape((width, HEAD_DIM), BF16)] + outs,
        in_specs=[FAR] * 3,
        out_specs=[WHOLE] * 3,
        scratch_shapes=[pltpu.VMEM((length, width), BF16)] * 3
        + [pltpu.SemaphoreType.DMA((2, blocks)), pltpu.SemaphoreType.DMA],
        compiler_params=pltpu.CompilerParams(vmem_limit_bytes=VMEM_LIMIT),
    )(*sources)


def out_kernel(heads, query_ref, first_inner_ref, second_inner_ref, up_ref, prior_ref, gain_ref, out_ref, sums_ref):
    def work(inner_ref):
        squares = jnp.zeros(sums_ref.shape[1:], F32)
        products = jnp.zeros(sums_ref.shape[1:], F32)
        for h in range(heads):
            out = inner_ref[:, columns(h)] + dot(query_ref[:, columns(h)], prior_ref[columns(h), :], (1, 0))
            out_ref[:, columns(h)] = out
            squares += out * out
            products += up_ref[:, columns(h)].astype(F32) * gain_ref[h][None] * out
        sums_ref[0] = squares
        sums_ref[1] = products

    first_core(lambda: work(first_inner_ref), lambda: work(second_inner_ref))


def token_factors(total_width, sums_refs):
    sums = functools.reduce(lambda a, b: a + b, [ref[...] for ref in sums_refs])
    inv = lax.rsqrt(jnp.sum(sums[0], axis=1, keepdims=True) / total_width + 1e-6)
    mean_dot = jnp.sum(sums[1], axis=1, keepdims=True) / total_width * inv
    return inv, mean_dot


def gain_rows(heads, parts):
    return -(-heads // parts)


def grad_out_kernel(heads, total_width, parts, *refs):
    out_ref, up_ref, gain_ref, query_ref, *sums_refs = refs[:-2]
    grad_ref, sent_ref = refs[-2:]
    inv, mean_dot = token_factors(total_width, sums_refs)
    rows = heads * HEAD_DIM // parts
    each = gain_rows(heads, parts)
    sent_ref[:, rows:, :] = jnp.zeros((parts, sent_ref.shape[1] - rows, HEAD_DIM), BF16)
    gains = []
    for h in range(heads):
        scaled = out_ref[:, columns(h)] * inv
        up = up_ref[:, columns(h)].astype(F32)
        grad = (inv * (up * gain_ref[h][None] - scaled * mean_dot)).astype(BF16)
        grad_ref[:, columns(h)] = grad
        state = dot(query_ref[:, columns(h)], grad, (0, 0)).astype(BF16)
        at = 0
        while at < HEAD_DIM:
            part, row = divmod(h * HEAD_DIM + at, rows)
            count = min(HEAD_DIM - at, rows - row)
            sent_ref[part, row:row + count, :] = state[at:at + count]
            at += count
        gains.append(jnp.sum(up * scaled, axis=0, keepdims=True))
        if h % each == each - 1 or h == heads - 1:
            part = h // each
            high, low = split(jnp.concatenate(gains, axis=0))
            sent_ref[part, rows:rows + len(gains), :] = high
            sent_ref[part, rows + each:rows + each + len(gains), :] = low
            gains = []


def inner_grads_kernel(span, done, query_ref, value_ref, grad_ref, weights_ref, scores_ref, inner_k_ref, inner_v_ref):
    mask = causal_mask(query_ref.shape[0])
    for h in span:
        cols = columns(h)
        scores = dot(grad_ref[:, cols], value_ref[:, cols], (1, 1))
        scores_ref[:, cols] = jnp.where(mask, scores, 0.0).astype(BF16)
    for h in span:
        cols = columns(h)
        inner_k_ref[:, cols] = dot(scores_ref[:, cols], query_ref[:, cols], (0, 0))
        inner_v_ref[:, cols] = dot(weights_ref[:, cols], grad_ref[:, cols], (0, 0))
        done(h)


def query_grads_kernel(total_width, span, done, *refs):
    scores_ref, key_ref, grad_ref, prior_ref, out_ref, gain_ref, *sums_refs = refs[:-2]
    attended_ref, grad_q_ref = refs[-2:]
    inv, _ = token_factors(total_width, sums_refs)
    for h in span:
        cols = columns(h)
        attended_ref[:, cols] = (out_ref[:, cols] * inv * gain_ref[h][None]).astype(BF16)
        grad_q = dot(scores_ref[:, cols], key_ref[:, cols], (1, 0)) + dot(grad_ref[:, cols], prior_ref[cols, :], (1, 1))
        grad_q_ref[:, cols] = grad_q.astype(BF16)
        done(h)


def last_grads_kernel(parts, first, span, done, *refs):
    key_ref, value_ref, got_ref, *inner_refs, gain_ref, grad_k_ref, grad_v_ref = refs
    inner_k_ref, inner_v_ref = inner_refs[:2] if first else inner_refs[2:]
    heads = len(span)
    rows = heads * HEAD_DIM // parts
    each = gain_rows(heads, parts)
    for h in span:
        cols = columns(h)
        pieces, at = [], 0
        while at < HEAD_DIM:
            part, row = divmod(h * HEAD_DIM + at, rows)
            count = min(HEAD_DIM - at, rows - row)
            pieces.append(got_ref[part, row:row + count, :])
            at += count
        later = pieces[0] if len(pieces) == 1 else jnp.concatenate(pieces, axis=0)
        grad_k = inner_k_ref[:, cols] + dot(value_ref[:, cols], later, (1, 1))
        grad_k_ref[:, cols] = grad_k.astype(BF16)
        grad_v = inner_v_ref[:, cols] + dot(key_ref[:, cols], later, (1, 0))
        grad_v_ref[:, cols] = grad_v.astype(BF16)
        done(h)
    for part in range(-(-heads // each)):
        pair = got_ref[part, rows:rows + 2 * each, :].astype(F32)
        own = min(each, heads - part * each)
        gain_ref[part * each:part * each + own, :] = pair[:own] + pair[each:each + own]


def gain_sum(rows, each, value):
    both = value[rows:rows + 2 * each, :]
    return both[:each] + both[each:]


def store_with_gain(ref, index, state, gain):
    rows, each = state.shape[0], gain.shape[0]
    high, low = split(gain)
    rest = jnp.zeros((ref.shape[-2] - rows - 2 * each, HEAD_DIM), F32)
    tail = jnp.concatenate([high.astype(F32), low.astype(F32), rest], axis=0).astype(BF16)
    ref[index + (slice(0, rows), slice(None))] = state.astype(BF16)
    ref[index + (slice(rows, None), slice(None))] = tail


def total_kernel(rows, each, got_ref, total_ref):
    total = jnp.sum(got_ref[...].astype(F32), axis=0)
    if each:
        store_with_gain(total_ref, (), total[:rows], gain_sum(rows, each, total))
    else:
        total_ref[...] = total.astype(BF16)


def running_kernel(rows, each, members, groups, reverse, *refs):
    got_ref, *total_refs, running_ref = refs
    group = lax.axis_index("seq") // members
    state = jnp.zeros((rows, HEAD_DIM), F32)
    for step, ref in enumerate(total_refs, 1):
        ahead = group + step < groups if reverse else group >= step
        state += jnp.where(ahead, ref[:rows, :].astype(F32), 0.0)
    if each:
        gain = gain_sum(rows, each, jnp.sum(got_ref[...].astype(F32), axis=0))
        for ref in total_refs:
            gain += gain_sum(rows, each, ref[...].astype(F32))
    order = member_order(members, reverse)
    for block in range(members - 1, -1, -1) if reverse else range(members):
        member = order.index(block)
        if each:
            store_with_gain(running_ref, (member,), state, gain)
        else:
            running_ref[member] = state.astype(BF16)
        state += got_ref[member, :rows, :].astype(F32)


def member_order(members, reverse):
    quick = (3, 2, 6, 4, 1, 0, 7, 5) if reverse else (3, 1, 6, 5, 7, 4, 0, 2)
    return list(quick if len(quick) == members else range(members))


def exclusive_sums(shares, rows, each, reverse, beside):
    count = lax.axis_size("seq")
    members = shares.shape[0]
    groups = count // members
    index_groups = [[g * members + block for block in member_order(members, reverse)] for g in range(groups)]
    exchange = functools.partial(
        lax.all_to_all, axis_name="seq", split_axis=0, concat_axis=0, axis_index_groups=index_groups, tiled=True
    )
    got = exchange(shares)
    totals = []
    if groups > 1:
        total = call(
            functools.partial(total_kernel, rows, each), shape(shares.shape[1:], BF16), got
        )
        for step in range(1, groups):
            hop = (-step if reverse else step) * members
            totals.append(lax.ppermute(total, "seq", [(i, (i + hop) % count) for i in range(count)]))
        got, work = beside(got, total)
    else:
        got, work = beside(got, got)
    running = call(
        functools.partial(running_kernel, rows, each, members, groups, reverse),
        shape(shares.shape, BF16), got, *totals,
    )
    return exchange(running), work


def sums_over_heads(sums):
    count = lax.axis_size("head")
    return [sums] + [
        lax.ppermute(sums, "head", [(i, (i + step) % count) for i in range(count)])
        for step in range(1, count)
    ]


def group_size(count):
    members = 1
    while members < 8 and count % (2 * members) == 0:
        members *= 2
    return members


def tied(value, after):
    return lax.optimization_barrier((value, after))[0]


def body(queries, key_vectors, value_vectors, norm_gain, upstream):
    length, width = queries.shape
    heads = width // HEAD_DIM
    total_width = width * lax.axis_size("head")
    members = group_size(lax.axis_size("seq"))
    rows = width // members
    gain = norm_gain.reshape(heads, HEAD_DIM)
    flat16 = shape((length, width), BF16)
    flat32 = shape((length, width), F32)
    flat_scores = shape((length, heads * length), BF16)

    every, none = range(heads), range(0)
    inner_out = functools.partial(inner_out_kernel, heads)
    state, weights, inner = local_states(heads, queries, key_vectors, value_vectors, [flat_scores, flat32])

    def inner_out_beside(got, total):
        results = call_on(
            False, inner_out, [flat_scores, flat32], tied(queries, total), key_vectors, value_vectors
        )
        return tied(got, results), results

    prior, (second_weights, second_inner) = exclusive_sums(
        state.reshape(members, rows, HEAD_DIM), rows, 0, False, inner_out_beside
    )
    prior = prior.reshape(width, HEAD_DIM)
    out, sums = call(
        functools.partial(out_kernel, heads),
        [flat32, shape((2, length, HEAD_DIM), F32)],
        queries, inner, second_inner, upstream, prior, gain,
    )
    sums = sums_over_heads(sums)
    each = gain_rows(heads, members)
    extra = -(-2 * each // 16) * 16
    grad, shares = call(
        functools.partial(grad_out_kernel, heads, total_width, members),
        [flat16, shape((members, rows + extra, HEAD_DIM), BF16)],
        out, upstream, gain, queries, *sums,
    )

    inner_shapes = [flat_scores, flat32, flat32]

    def query_grads(spans, after, scores, held=(), blocks=4):
        return leaving(
            [functools.partial(query_grads_kernel, total_width)] * 2, spans,
            [scores, key_vectors, tied(grad, after), prior, out, gain, *sums], [flat16, flat16], (), held, blocks,
        )

    second_scores, *second_inner = leaving(
        [inner_grads_kernel] * 2, (none, every),
        [tied(queries, shares), value_vectors, grad, second_weights], inner_shapes, (), (), 8,
    )
    held = query_grads((none, every), second_inner, second_scores, (), 1)
    shares = tied(shares, held)

    def grads_beside(got, total):
        scores, *inner = call_on(
            True, functools.partial(inner_grads_kernel, every, lambda h: None), inner_shapes,
            tied(queries, total), value_vectors, grad, weights,
        )
        results = query_grads((every, none), inner, scores, held)
        return tied(got, results), (inner, results)

    later, (inner, (attended, grad_q)) = exclusive_sums(shares, rows, each, True, grads_beside)
    grad_k, grad_v, grad_gain = leaving(
        [functools.partial(last_grads_kernel, members, first) for first in (True, False)], (every, every),
        [key_vectors, value_vectors, later, *inner, *second_inner],
        [flat16, flat16], [shape((heads, HEAD_DIM), F32)], (), 6
    )
    return attended, grad_q, grad_k, grad_v, grad_gain.reshape(-1)


def solution(mesh):
    split_both = P("seq", "head")
    in_specs = (split_both, split_both, split_both, P("head"), split_both)
    out_specs = (split_both, split_both, split_both, split_both, P("head"))
    return jax.shard_map(body, mesh=mesh, in_specs=in_specs, out_specs=out_specs, check_vma=False)
```

```python
import functools

import jax
import jax.numpy as jnp
from jax import lax
from jax.experimental import pallas as pl
from jax.experimental.pallas import tpu as pltpu
from jax.sharding import PartitionSpec as P

HEAD_DIM = 128
F32 = jnp.float32
BF16 = jnp.bfloat16
VMEM_LIMIT = 40 * 1024 * 1024
WHOLE = pl.BlockSpec(memory_space=pltpu.VMEM)
FAR = pl.BlockSpec(memory_space=pltpu.HBM)


def shape(dims, dtype):
    return jax.ShapeDtypeStruct(dims, dtype)


def call(kernel, out_shape, *args):
    return pl.pallas_call(
        kernel,
        out_shape=out_shape,
        in_specs=[WHOLE] * len(args),
        out_specs=jax.tree.map(lambda _: WHOLE, out_shape),
        compiler_params=pltpu.CompilerParams(vmem_limit_bytes=VMEM_LIMIT),
    )(*args)


def first_core(mine, other):
    odd = lax.axis_index("head") % 2
    pl.when(odd == 0)(mine)
    pl.when(odd == 1)(other)


def call_on(first, kernel, out_shape, *args):
    def whole(*refs):
        work, rest = lambda: kernel(*refs), lambda: None
        first_core(work if first else rest, rest if first else work)

    return call(whole, out_shape, *args)


def dot(a, b, over):
    return lax.dot_general(a, b, ((over[:1], over[1:]), ((), ())), preferred_element_type=F32)


def split(value):
    high = value.astype(BF16)
    return high, (value - high.astype(F32)).astype(BF16)


def columns(head):
    return pl.ds(head * HEAD_DIM, HEAD_DIM)


def causal_mask(length):
    rows = lax.broadcasted_iota(jnp.int32, (length, length), 0)
    cols = lax.broadcasted_iota(jnp.int32, (length, length), 1)
    return cols <= rows


def leave(kernel, span, ins, outs, buffers, sems, blocks):
    if not span:
        return
    step = -(-len(span) // blocks)
    copies = []

    def done(h):
        place = h - span.start
        if place % step == step - 1 or h == span[-1]:
            first = span.start + place // step * step
            cols = pl.ds(first * HEAD_DIM, (h + 1 - first) * HEAD_DIM)
            for i, (out, buffer) in enumerate(zip(outs, buffers)):
                copy = pltpu.make_async_copy(buffer.at[:, cols], out.at[:, cols], sems.at[place // step, i])
                copy.start()
                copies.append(copy)

    kernel(span, done, *ins, *buffers)
    for copy in copies:
        copy.wait()


def leaving(kernels, spans, ins, outs, near_outs=(), held=(), blocks=4):
    count = len(outs)

    def whole(*refs):
        in_refs, refs = refs[:len(ins)], refs[len(ins) + len(held):]
        out_refs, refs = refs[:count], refs[count:]
        near_refs, refs = refs[:len(near_outs)], refs[len(near_outs):]
        buffers, sems = refs[:count], refs[count]
        work = [
            functools.partial(leave, kernel, span, in_refs + near_refs, out_refs, buffers, sems, blocks)
            for kernel, span in zip(kernels, spans)
        ]
        first_core(*work)

    return pl.pallas_call(
        whole,
        out_shape=list(outs) + list(near_outs),
        in_specs=[WHOLE] * len(ins) + [FAR] * len(held),
        out_specs=[FAR] * count + [WHOLE] * len(near_outs),
        scratch_shapes=[pltpu.VMEM(a.shape, a.dtype) for a in outs] + [pltpu.SemaphoreType.DMA((blocks, count))],
        input_output_aliases={len(ins) + i: i for i in range(len(held))},
        compiler_params=pltpu.CompilerParams(vmem_limit_bytes=VMEM_LIMIT),
    )(*ins, *held)


def inner_out_kernel(heads, query_ref, key_ref, value_ref, weights_ref, inner_ref):
    mask = causal_mask(query_ref.shape[0])
    for h in range(heads):
        scores = dot(query_ref[:, columns(h)], key_ref[:, columns(h)], (1, 1))
        weights_ref[:, columns(h)] = jnp.where(mask, scores, 0.0).astype(BF16)
    for h in range(heads):
        inner_ref[:, columns(h)] = dot(weights_ref[:, columns(h)], value_ref[:, columns(h)], (1, 0))


def local_states(heads, queries, key_vectors, value_vectors, outs, blocks=2):
    length, width = key_vectors.shape
    while heads % blocks:
        blocks -= 1
    step = heads // blocks
    sources = [pltpu.with_memory_space_constraint(a, pltpu.HBM) for a in (key_vectors, value_vectors, queries)]

    def whole(*refs):
        far, (state_ref, *out_refs) = refs[:3], refs[3:6]
        key_ref, value_ref, query_ref, sems, query_sem = refs[6:]
        arrivals = []
        for block in range(blocks):
            cols = pl.ds(block * step * HEAD_DIM, step * HEAD_DIM)
            for i, (ref, buffer) in enumerate(((far[0], key_ref), (far[1], value_ref))):
                arrivals.append(pltpu.make_async_copy(ref.at[:, cols], buffer.at[:, cols], sems.at[i, block]))
        query_copy = pltpu.make_async_copy(far[2], query_ref, query_sem)
        for copy in arrivals:
            copy.start()
        first_core(query_copy.start, lambda: None)
        for h in range(heads):
            if h % step == 0:
                for copy in arrivals[2 * (h // step):2 * (h // step) + 2]:
                    copy.wait()
            part = dot(key_ref[:, columns(h)], value_ref[:, columns(h)], (0, 0))
            state_ref[columns(h), :] = part.astype(BF16)

        def early():
            query_copy.wait()
            inner_out_kernel(heads, query_ref, key_ref, value_ref, *out_refs)

        first_core(early, lambda: None)

    return pl.pallas_call(
        whole,
        out_shape=[shape((width, HEAD_DIM), BF16)] + outs,
        in_specs=[FAR] * 3,
        out_specs=[WHOLE] * 3,
        scratch_shapes=[pltpu.VMEM((length, width), BF16)] * 3
        + [pltpu.SemaphoreType.DMA((2, blocks)), pltpu.SemaphoreType.DMA],
        compiler_params=pltpu.CompilerParams(vmem_limit_bytes=VMEM_LIMIT),
    )(*sources)


def out_kernel(heads, query_ref, first_inner_ref, second_inner_ref, up_ref, prior_ref, gain_ref, out_ref, sums_ref):
    def work(inner_ref):
        squares = jnp.zeros(sums_ref.shape, F32)
        products = jnp.zeros(sums_ref.shape, F32)
        for h in range(heads):
            out = inner_ref[:, columns(h)] + dot(query_ref[:, columns(h)], prior_ref[columns(h), :], (1, 0))
            out_ref[:, columns(h)] = out
            squares += out * out
            products += up_ref[:, columns(h)].astype(F32) * gain_ref[h][None] * out
        half = HEAD_DIM // 2
        fold = lambda value: value[:, :half] + value[:, half:]
        sums_ref[...] = jnp.concatenate([fold(squares), fold(products)], axis=1)

    first_core(lambda: work(first_inner_ref), lambda: work(second_inner_ref))


def token_factors(total_width, sums_refs):
    sums = functools.reduce(lambda a, b: a + b, [ref[...] for ref in sums_refs])
    inv = lax.rsqrt(jnp.sum(sums[:, :HEAD_DIM // 2], axis=1, keepdims=True) / total_width + 1e-6)
    mean_dot = jnp.sum(sums[:, HEAD_DIM // 2:], axis=1, keepdims=True) / total_width * inv
    return inv, mean_dot


def gain_rows(heads, parts):
    return -(-heads // parts)


def grad_out_kernel(heads, total_width, parts, *refs):
    out_ref, up_ref, gain_ref, query_ref, *sums_refs = refs[:-2]
    grad_ref, sent_ref = refs[-2:]
    inv, mean_dot = token_factors(total_width, sums_refs)
    rows = heads * HEAD_DIM // parts
    each = gain_rows(heads, parts)
    sent_ref[:, rows:, :] = jnp.zeros((parts, sent_ref.shape[1] - rows, HEAD_DIM), BF16)
    gains = []
    for h in range(heads):
        scaled = out_ref[:, columns(h)] * inv
        up = up_ref[:, columns(h)].astype(F32)
        grad = (inv * (up * gain_ref[h][None] - scaled * mean_dot)).astype(BF16)
        grad_ref[:, columns(h)] = grad
        state = dot(query_ref[:, columns(h)], grad, (0, 0)).astype(BF16)
        at = 0
        while at < HEAD_DIM:
            part, row = divmod(h * HEAD_DIM + at, rows)
            count = min(HEAD_DIM - at, rows - row)
            sent_ref[part, row:row + count, :] = state[at:at + count]
            at += count
        gains.append(jnp.sum(up * scaled, axis=0, keepdims=True))
        if h % each == each - 1 or h == heads - 1:
            part = h // each
            high, low = split(jnp.concatenate(gains, axis=0))
            sent_ref[part, rows:rows + len(gains), :] = high
            sent_ref[part, rows + each:rows + each + len(gains), :] = low
            gains = []


def inner_grads_kernel(span, done, query_ref, value_ref, grad_ref, weights_ref, scores_ref, inner_k_ref, inner_v_ref):
    mask = causal_mask(query_ref.shape[0])
    for h in span:
        cols = columns(h)
        scores = dot(grad_ref[:, cols], value_ref[:, cols], (1, 1))
        scores_ref[:, cols] = jnp.where(mask, scores, 0.0).astype(BF16)
    for h in span:
        cols = columns(h)
        inner_k_ref[:, cols] = dot(scores_ref[:, cols], query_ref[:, cols], (0, 0))
        inner_v_ref[:, cols] = dot(weights_ref[:, cols], grad_ref[:, cols], (0, 0))
        done(h)


def query_grads_kernel(total_width, span, done, *refs):
    scores_ref, key_ref, grad_ref, prior_ref, out_ref, gain_ref, *sums_refs = refs[:-2]
    attended_ref, grad_q_ref = refs[-2:]
    inv, _ = token_factors(total_width, sums_refs)
    for h in span:
        cols = columns(h)
        attended_ref[:, cols] = (out_ref[:, cols] * inv * gain_ref[h][None]).astype(BF16)
        grad_q = dot(scores_ref[:, cols], key_ref[:, cols], (1, 0)) + dot(grad_ref[:, cols], prior_ref[cols, :], (1, 1))
        grad_q_ref[:, cols] = grad_q.astype(BF16)
        done(h)


def last_grads_kernel(parts, first, span, done, *refs):
    key_ref, value_ref, got_ref, *inner_refs, gain_ref, grad_k_ref, grad_v_ref = refs
    inner_k_ref, inner_v_ref = inner_refs[:2] if first else inner_refs[2:]
    heads = len(span)
    rows = heads * HEAD_DIM // parts
    each = gain_rows(heads, parts)
    for h in span:
        cols = columns(h)
        pieces, at = [], 0
        while at < HEAD_DIM:
            part, row = divmod(h * HEAD_DIM + at, rows)
            count = min(HEAD_DIM - at, rows - row)
            pieces.append(got_ref[part, row:row + count, :])
            at += count
        later = pieces[0] if len(pieces) == 1 else jnp.concatenate(pieces, axis=0)
        grad_k = inner_k_ref[:, cols] + dot(value_ref[:, cols], later, (1, 1))
        grad_k_ref[:, cols] = grad_k.astype(BF16)
        grad_v = inner_v_ref[:, cols] + dot(key_ref[:, cols], later, (1, 0))
        grad_v_ref[:, cols] = grad_v.astype(BF16)
        done(h)
    for part in range(-(-heads // each)):
        pair = got_ref[part, rows:rows + 2 * each, :].astype(F32)
        own = min(each, heads - part * each)
        gain_ref[part * each:part * each + own, :] = pair[:own] + pair[each:each + own]


def gain_sum(rows, each, value):
    both = value[rows:rows + 2 * each, :]
    return both[:each] + both[each:]


def store_with_gain(ref, index, state, gain):
    rows, each = state.shape[0], gain.shape[0]
    high, low = split(gain)
    rest = jnp.zeros((ref.shape[-2] - rows - 2 * each, HEAD_DIM), F32)
    tail = jnp.concatenate([high.astype(F32), low.astype(F32), rest], axis=0).astype(BF16)
    ref[index + (slice(0, rows), slice(None))] = state.astype(BF16)
    ref[index + (slice(rows, None), slice(None))] = tail


def total_kernel(rows, each, got_ref, total_ref):
    total = jnp.sum(got_ref[...].astype(F32), axis=0)
    if each:
        store_with_gain(total_ref, (), total[:rows], gain_sum(rows, each, total))
    else:
        total_ref[...] = total.astype(BF16)


def running_kernel(rows, each, members, groups, reverse, *refs):
    got_ref, *total_refs, running_ref = refs
    group = lax.axis_index("seq") // members
    state = jnp.zeros((rows, HEAD_DIM), F32)
    for step, ref in enumerate(total_refs, 1):
        ahead = group + step < groups if reverse else group >= step
        state += jnp.where(ahead, ref[:rows, :].astype(F32), 0.0)
    if each:
        gain = gain_sum(rows, each, jnp.sum(got_ref[...].astype(F32), axis=0))
        for ref in total_refs:
            gain += gain_sum(rows, each, ref[...].astype(F32))
    order = member_order(members)
    for block in range(members - 1, -1, -1) if reverse else range(members):
        member = order.index(block)
        if each:
            store_with_gain(running_ref, (member,), state, gain)
        else:
            running_ref[member] = state.astype(BF16)
        state += got_ref[member, :rows, :].astype(F32)


def member_order(members):
    quick = (3, 1, 5, 6, 7, 4, 0, 2)
    return list(quick if len(quick) == members else range(members))


def exclusive_sums(shares, rows, each, reverse, beside):
    count = lax.axis_size("seq")
    members = shares.shape[0]
    groups = count // members
    index_groups = [[g * members + block for block in member_order(members)] for g in range(groups)]
    exchange = functools.partial(
        lax.all_to_all, axis_name="seq", split_axis=0, concat_axis=0, axis_index_groups=index_groups, tiled=True
    )
    got = exchange(shares)
    totals = []
    if groups > 1:
        total = call(
            functools.partial(total_kernel, rows, each), shape(shares.shape[1:], BF16), got
        )
        for step in range(1, groups):
            hop = (-step if reverse else step) * members
            totals.append(lax.ppermute(total, "seq", [(i, (i + hop) % count) for i in range(count)]))
        got, work = beside(got, total)
    else:
        got, work = beside(got, got)
    running = call(
        functools.partial(running_kernel, rows, each, members, groups, reverse),
        shape(shares.shape, BF16), got, *totals,
    )
    return exchange(running), work


def sums_over_heads(sums):
    count = lax.axis_size("head")
    return [sums] + [
        lax.ppermute(sums, "head", [(i, (i + step) % count) for i in range(count)])
        for step in range(1, count)
    ]


def group_size(count):
    members = 1
    while members < 8 and count % (2 * members) == 0:
        members *= 2
    return members


def tied(value, after):
    return lax.optimization_barrier((value, after))[0]


def body(queries, key_vectors, value_vectors, norm_gain, upstream):
    length, width = queries.shape
    heads = width // HEAD_DIM
    total_width = width * lax.axis_size("head")
    members = group_size(lax.axis_size("seq"))
    rows = width // members
    gain = norm_gain.reshape(heads, HEAD_DIM)
    flat16 = shape((length, width), BF16)
    flat32 = shape((length, width), F32)
    flat_scores = shape((length, heads * length), BF16)

    every, none = range(heads), range(0)
    inner_out = functools.partial(inner_out_kernel, heads)
    state, weights, inner = local_states(heads, queries, key_vectors, value_vectors, [flat_scores, flat32])

    def inner_out_beside(got, total):
        results = call_on(
            False, inner_out, [flat_scores, flat32], tied(queries, total), key_vectors, value_vectors
        )
        return tied(got, results), results

    prior, (second_weights, second_inner) = exclusive_sums(
        state.reshape(members, rows, HEAD_DIM), rows, 0, False, inner_out_beside
    )
    prior = prior.reshape(width, HEAD_DIM)
    out, sums = call(
        functools.partial(out_kernel, heads),
        [flat32, shape((length, HEAD_DIM), F32)],
        queries, inner, second_inner, upstream, prior, gain,
    )
    sums = sums_over_heads(sums)
    each = gain_rows(heads, members)
    extra = -(-2 * each // 16) * 16
    grad, shares = call(
        functools.partial(grad_out_kernel, heads, total_width, members),
        [flat16, shape((members, rows + extra, HEAD_DIM), BF16)],
        out, upstream, gain, queries, *sums,
    )

    inner_shapes = [flat_scores, flat32, flat32]

    def query_grads(spans, after, scores, held=(), blocks=4):
        return leaving(
            [functools.partial(query_grads_kernel, total_width)] * 2, spans,
            [scores, key_vectors, tied(grad, after), prior, out, gain, *sums], [flat16, flat16], (), held, blocks,
        )

    second_scores, *second_inner = leaving(
        [inner_grads_kernel] * 2, (none, every),
        [tied(queries, shares), value_vectors, grad, second_weights], inner_shapes, (), (), 8,
    )
    held = query_grads((none, every), second_inner, second_scores, (), 1)
    shares = tied(shares, held)

    def grads_beside(got, total):
        scores, *inner = call_on(
            True, functools.partial(inner_grads_kernel, every, lambda h: None), inner_shapes,
            tied(queries, total), value_vectors, grad, weights,
        )
        results = query_grads((every, none), inner, scores, held)
        return tied(got, results), (inner, results)

    later, (inner, (attended, grad_q)) = exclusive_sums(shares, rows, each, True, grads_beside)
    grad_k, grad_v, grad_gain = leaving(
        [functools.partial(last_grads_kernel, members, first) for first in (True, False)], (every, every),
        [key_vectors, value_vectors, later, *inner, *second_inner],
        [flat16, flat16], [shape((heads, HEAD_DIM), F32)], (), 6
    )
    return attended, grad_q, grad_k, grad_v, grad_gain.reshape(-1)


def solution(mesh):
    split_both = P("seq", "head")
    in_specs = (split_both, split_both, split_both, P("head"), split_both)
    out_specs = (split_both, split_both, split_both, split_both, P("head"))
    return jax.shard_map(body, mesh=mesh, in_specs=in_specs, out_specs=out_specs, check_vma=False)
```
